32 devices in a mesh: batch: 4 (over y, x), row: 2 (over core), col: 4 (over z).
Axes of the slice: x: 2, y: 2, z: 4, core: 2. Of those that a mesh axis runs over, the one named last changes fastest.
Arguments:
- tokens: bfloat16 [4096, 6144], P('batch', 'row'), may hold values from -6 to 6
- cotangent: bfloat16 [4096, 6144], P('batch', 'row'), may hold values from -1.5 to 1.5
- weight_in: bfloat16 [6144, 12288], P('row', 'col'), may hold values from -0.078125 to 0.078125
- weight_out: bfloat16 [12288, 6144], P('col', 'row'), may hold values from -0.0546875 to 0.0546875
- segment_ids: int32 [4096], P('batch'), may hold values from 0 to 31, as said below
- keep_mask: int32 [4096], P('batch'), may hold values 0 or 1
Outputs:
- grad_tokens: bfloat16 [4096, 6144], P('batch', 'row')
- grad_weight_in: bfloat16 [6144, 12288], P(('row', 'batch'), 'col')
- grad_weight_out: bfloat16 [12288, 6144], P('col', ('row', 'batch'))
The draws below stay inside these ranges and needn't reach their ends.
Inputs may be any that keep to these rules, and one draw needn't show every extreme that they name: `segment_ids`: never falling along the bin; every image 0 .. 31 has 1 to 192 tokens, and some image has exactly 192.
All inputs are finite; a program needn't handle non-finite values. No bound on the sum of `keep_mask` on one device may be relied on, other than what follows from the above.
Results may differ from the reference program's by a relative error of at most 0.023.
Values may be sent and summed in bfloat16 or wider, within the bound.
No kernel may reach another device: no remote copies, remote signals or barrier semaphores. Data moves between devices by JAX's collectives and lax.ppermute only.
A program may use at most 192 MiB of HBM per device.

```python
import jax
import jax.numpy as jnp
from jax import lax

D = 6144
FF = 12288
TOKENS = 4096
SEGS = 32
IMAGE_MEAN = 128
N_BATCH = 4
N_ROW = 2
N_COL = 4


def draw_segment_ids(key, part):
    jitter_key = jax.random.fold_in(key, 17)
    count = SEGS - 1
    index = jnp.arange(count, dtype=jnp.int32)
    jitter_width = IMAGE_MEAN // 8
    jitter = jax.random.randint(jitter_key, (count,), -jitter_width, jitter_width + 1, dtype=jnp.int32)
    jitter = jnp.where(index == count - 1, 0, jitter)
    cuts = index * IMAGE_MEAN + IMAGE_MEAN // 2 + jitter
    places = jnp.arange(TOKENS, dtype=jnp.int32)
    return jnp.sum((places[:, None] >= cuts[None, :]).astype(jnp.int32), axis=1).astype(jnp.int32)


def set_ends(result, rng, smallest, high):
    shape = result.shape
    place = [jax.random.randint(jax.random.fold_in(rng, axis), (), 0, shape[axis]) for axis in range(len(shape))]
    result = result.at[tuple(place)].set(smallest)
    longest = shape.index(max(shape))
    place[longest] = (place[longest] + 1) % shape[longest]
    return result.at[tuple(place)].set(high)


def block_scale(key, dims, pieces, smallest, top_value):
    def one(axis_at, parts):
        steps = jax.random.uniform(jax.random.fold_in(jax.random.fold_in(key, 6), axis_at), (parts,), jnp.float32, smallest / len(pieces), top_value / len(pieces))
        return jnp.repeat(jnp.exp(steps), dims[axis_at] // parts).reshape((-1,) + (1,) * (len(dims) - axis_at - 1))

    factor_of = one(*pieces[0])
    for cut in pieces[1:]:
        factor_of = factor_of * one(*cut)
    return factor_of


def gaussian(rng, dims, deviation, bound, pieces=(), kind=jnp.bfloat16):
    gain = block_scale(rng, dims, pieces, -0.22, 0.18) if pieces else 1.0
    entries = jax.random.normal(rng, dims, jnp.float32) * deviation * gain
    return jnp.minimum(jnp.maximum(entries, -bound), bound).astype(kind)


def setup_inputs(seed: int = 0) -> dict:
    key_of = jax.random.split(jax.random.key(seed), 7)
    return {
        "tokens": gaussian(key_of[0], (TOKENS, D), 1.0, 6.0, ((0, 4), (1, 2))),
        "cotangent": gaussian(key_of[1], (TOKENS, D), 0.25, 1.5, ((0, 4), (1, 2))),
        "weight_in": gaussian(key_of[2], (D, FF), D ** -0.5, 0.078125, ((0, 2), (1, 4))),
        "weight_out": gaussian(key_of[3], (FF, D), FF ** -0.5, 0.0546875, ((0, 4), (1, 2))),
        "segment_ids": draw_segment_ids(jax.random.fold_in(key_of[6], 71), 0),
        "keep_mask": set_ends((jax.random.randint(key_of[5], (TOKENS,), 0, 8) < 7).astype(jnp.int32), jax.random.fold_in(key_of[5], 1), 0, 1),
    }


inv_root_two = 0.7071067811865476
inv_root_tau = 0.3989422804014327

def add_rounded(total, term):
    return total + lax.optimization_barrier(term.astype(jnp.bfloat16)).astype(jnp.float32)

def contract_cols(left, right):
    return lax.dot_general(left, right, (((1,), (1,)), ((), ())), preferred_element_type=jnp.float32)

def contract_rows(left, right):
    return lax.dot_general(left, right, (((0,), (0,)), ((), ())), preferred_element_type=jnp.float32)

def reference(tokens, cotangent, weight_in, weight_out, segment_ids, keep_mask):
    labels = jnp.arange(SEGS, dtype=jnp.int32)
    onehot = (segment_ids[:, None] == labels[None, :]).astype(jnp.float32)
    keeping = keep_mask.astype(jnp.float32)
    image_sizes = lax.optimization_barrier(jnp.sum(onehot * keeping[:, None], axis=0))
    per_token = jnp.dot(onehot, image_sizes, precision=lax.Precision.HIGHEST)
    token_weight = keeping * jnp.sqrt(IMAGE_MEAN / jnp.maximum(per_token, 1.0))
    scaled = (cotangent.astype(jnp.float32) * token_weight[:, None]).astype(jnp.bfloat16)
    width_block = D // N_ROW
    pre_act = jnp.zeros((TOKENS, FF), jnp.float32)
    back_grad = jnp.zeros((TOKENS, FF), jnp.float32)
    for bucket in range(N_ROW):
        lower = bucket * width_block
        upper = lower + width_block
        pre_act = add_rounded(pre_act, jnp.dot(tokens[:, lower:upper], weight_in[lower:upper, :], preferred_element_type=jnp.float32))
        back_grad = add_rounded(back_grad, contract_cols(scaled[:, lower:upper], weight_out[:, lower:upper]))
    normal_cdf = 0.5 * (1.0 + lax.erf(pre_act * inv_root_two))
    activation = (pre_act * normal_cdf).astype(jnp.bfloat16)
    slopes = normal_cdf + pre_act * jnp.exp(-0.5 * pre_act * pre_act) * inv_root_tau
    hidden_grad = (back_grad * slopes).astype(jnp.bfloat16)
    hidden_block = FF // N_COL
    grad_tokens = jnp.zeros((TOKENS, D), jnp.float32)
    for bucket in range(N_COL):
        lower = bucket * hidden_block
        upper = lower + hidden_block
        grad_tokens = add_rounded(grad_tokens, contract_cols(hidden_grad[:, lower:upper], weight_in[:, lower:upper]))
    token_block = TOKENS // N_BATCH
    grad_in = jnp.zeros((D, FF), jnp.float32)
    grad_out = jnp.zeros((FF, D), jnp.float32)
    for bucket in range(N_BATCH):
        lower = bucket * token_block
        upper = lower + token_block
        grad_in = add_rounded(grad_in, contract_rows(tokens[lower:upper], hidden_grad[lower:upper]))
        grad_out = add_rounded(grad_out, contract_rows(activation[lower:upper], scaled[lower:upper]))
    return (grad_tokens.astype(jnp.bfloat16), grad_in.astype(jnp.bfloat16), grad_out.astype(jnp.bfloat16))
```

```python
import functools

import jax
import jax.numpy as jnp
from jax import lax
from jax.experimental import pallas as pl
from jax.experimental.pallas import tpu as pltpu
from jax.sharding import PartitionSpec as P

SEGS = 32
IMAGE_MEAN = 128
VMEM_BYTES = 60 * 2**20
FF_CHUNKS = 2
PIECES = 8
PIECE_CALL = 2
LINE_STEPS = 2
PICKED = 1


inv_root_two = 0.7071067811865476
inv_root_tau = 0.3989422804014327


def padded(x, sides, width):
    for axis, dim in sides:
        size, length = (lax.axis_size(axis), x.shape[dim])
        up = [(i, (i + 1) % size) for i in range(size - 1)]
        down = [(j, i) for i, j in up]
        last = lax.slice_in_dim(x, length - width, length, axis=dim)
        first = lax.slice_in_dim(x, 0, width, axis=dim)
        before = lax.ppermute(last, axis, up)
        after = lax.ppermute(first, axis, down)
        x = jnp.concatenate([before, x, after], axis=dim)
    return x


def gelu_parts(pre_act):
    normal_cdf = 0.5 * (1.0 + lax.erf(pre_act * inv_root_two))
    slopes = normal_cdf + pre_act * jnp.exp(-0.5 * pre_act * pre_act) * inv_root_tau
    return (pre_act * normal_cdf, slopes)


def contract_cols(left, right):
    return lax.dot_general(
        left, right, (((1,), (1,)), ((), ())), preferred_element_type=jnp.float32
    )


def contract_rows(left, right):
    return lax.dot_general(
        left, right, (((0,), (0,)), ((), ())), preferred_element_type=jnp.float32
    )


def image_weights(segment_ids, keep_mask):
    labels = jnp.arange(SEGS, dtype=jnp.int32)
    onehot = (segment_ids[:, None] == labels[None, :]).astype(jnp.float32)
    keeping = keep_mask.astype(jnp.float32)
    local_sizes = jnp.sum(onehot * keeping[:, None], axis=0)
    beside = padded(local_sizes[None, :], (("batch", 0),), 1)
    image_sizes = jnp.sum(beside, axis=0)
    per_token = jnp.dot(onehot, image_sizes, precision=lax.Precision.HIGHEST)
    return keeping * jnp.sqrt(IMAGE_MEAN / jnp.maximum(per_token, 1.0))


def per_device_any(tokens, cotangent, weight_in, weight_out, segment_ids, keep_mask):
    token_weight = image_weights(segment_ids, keep_mask)
    scaled = (cotangent.astype(jnp.float32) * token_weight[:, None]).astype(jnp.bfloat16)
    hidden_cols = weight_in.shape[1]
    forward_rows = jnp.dot(tokens, weight_in, preferred_element_type=jnp.float32)
    backward_rows = contract_cols(scaled, weight_out)
    summed = lax.psum_scatter(
        jnp.concatenate([forward_rows, backward_rows], axis=1).astype(jnp.bfloat16),
        "row",
        scatter_dimension=0,
        tiled=True,
    ).astype(jnp.float32)
    act_share, slope_share = gelu_parts(summed[:, :hidden_cols])
    grad_share = (summed[:, hidden_cols:] * slope_share).astype(jnp.bfloat16)
    activation, hidden_grad = (
        lax.all_gather(act_share.astype(jnp.bfloat16), "row", axis=0, tiled=True),
        lax.all_gather(grad_share, "row", axis=0, tiled=True),
    )
    input_part = contract_cols(hidden_grad, weight_in)
    grad_tokens = lax.psum(input_part.astype(jnp.bfloat16), "col")
    first_grad = contract_rows(tokens, hidden_grad)
    second_grad = contract_rows(scaled, activation)
    summed_grads = lax.psum_scatter(
        jnp.concatenate([first_grad, second_grad], axis=1).astype(jnp.bfloat16),
        "batch",
        scatter_dimension=0,
        tiled=True,
    ).astype(jnp.float32)
    grad_in = summed_grads[:, :hidden_cols].astype(jnp.bfloat16)
    grad_out = summed_grads[:, hidden_cols:].T.astype(jnp.bfloat16)
    return (grad_tokens, grad_in, grad_out)


def low(x):
    return x.astype(jnp.bfloat16)


def wide(x):
    return x.astype(jnp.float32)


def swap(x, axis, mask):
    size = lax.axis_size(axis)
    return lax.ppermute(x, axis, [(i, i ^ mask) for i in range(size)])


def call(kernel, outs, grid, in_specs, out_specs, scratch=(), scalars=1, aliases=None):
    def run(args, after):
        first, waits, results = len(in_specs) + scalars, len(after), len(outs)

        def body(*refs):
            refs = refs[:first] + refs[first + waits :]
            kernel(*refs[: first + results], *refs[first + results + 1 :])

        anywhere = pl.BlockSpec(memory_space=pl.ANY)
        return pl.pallas_call(
            body,
            out_shape=[jax.ShapeDtypeStruct(shape, jnp.bfloat16) for shape in [*outs, (16, 128)]],
            grid_spec=pltpu.PrefetchScalarGridSpec(
                num_scalar_prefetch=scalars,
                grid=grid,
                in_specs=[*in_specs] + [anywhere] * waits,
                out_specs=[*out_specs, anywhere],
                scratch_shapes=list(scratch),
            ),
            input_output_aliases=aliases or {},
            compiler_params=pltpu.CompilerParams(vmem_limit_bytes=VMEM_BYTES, has_side_effects=True),
            cost_estimate=pl.CostEstimate(flops=0, bytes_accessed=0, transcendentals=0),
        )(*args, *after)

    return run


def start_all(copies):
    for copy in copies:
        copy.start()
    for copy in copies:
        copy.wait()


def pick_kernel(each, place, left, right, *refs):
    step = pl.program_id(0)
    pieces = len(refs) // 2
    for piece in range(pieces):

        @pl.when(step // each == piece)
        def _(piece=piece):
            refs[piece][...] = left[...]
            refs[pieces + piece][...] = right[...]


def pick_columns(after, place, left, right, left_offsets, right_offsets, block, pieces, tile):
    rows = left.shape[0]
    tiles = block // tile
    width = block * len(left_offsets)
    each = width // tile // pieces

    def source(offsets):
        def index(j, place):
            offset = offsets[-1]
            for i in reversed(range(len(offsets) - 1)):
                offset = jnp.where(j < (i + 1) * tiles, offsets[i], offset)
            return (0, (place[1] ^ offset) * tiles + j % tiles)

        return pl.BlockSpec((rows, tile), index)

    def target(piece):
        return pl.BlockSpec((rows, tile), lambda j, place: (0, jnp.clip(j - piece * each, 0, each - 1)))

    return call(
        functools.partial(pick_kernel, each),
        [(rows, width // pieces)] * (2 * pieces),
        (width // tile,),
        [source(left_offsets), source(right_offsets)],
        [target(i) for i in range(pieces)] * 2,
    )((place, left, right), after)


def partial_kernel(
    steps, place, left, right, weight_in, weight_out, own_pre, own_back, sent_pre, sent_back, held_left, held_right, sems
):
    step = pl.program_id(0)
    share = own_pre.shape[0]
    copies = [
        pltpu.make_async_copy(left, held_left, sems.at[0]),
        pltpu.make_async_copy(right, held_right, sems.at[1]),
    ]

    def store(product, own, sent):
        mine = place[0] == 0
        own[...] = low(jnp.where(mine, product[:share], product[share:]))
        sent[...] = low(jnp.where(mine, product[share:], product[:share]))

    @pl.when(step == 0)
    def _():
        copies[0].start()
        copies[1].start()
        copies[0].wait()

    @pl.when(step == steps)
    def _():
        copies[1].wait()

    @pl.when(step < steps)
    def _():
        store(jnp.dot(held_left[...], weight_in[...], preferred_element_type=jnp.float32), own_pre, sent_pre)

    @pl.when(step >= steps)
    def _():
        store(contract_cols(held_right[...], weight_out[...]), own_back, sent_back)


def partial_products(after, place, left, right, weight_in, weight_out, index, chunk, tile):
    rows, width = left.shape
    steps = chunk // tile
    early = pl.BlockSpec((rows // 2, tile), lambda j, c: (0, jnp.minimum(j, steps - 1)))
    late = pl.BlockSpec((rows // 2, tile), lambda j, c: (0, jnp.maximum(j - steps, 0)))
    return call(
        functools.partial(partial_kernel, steps),
        [(rows // 2, chunk)] * 4,
        (2 * steps,),
        [
            pl.BlockSpec(memory_space=pl.ANY),
            pl.BlockSpec(memory_space=pl.ANY),
            pl.BlockSpec((width, tile), lambda j, c: (0, index * steps + jnp.minimum(j, steps - 1))),
            pl.BlockSpec((tile, width), lambda j, c: (index * steps + jnp.maximum(j - steps, 0), 0)),
        ],
        [early, late, early, late],
        [
            pltpu.VMEM((rows, width), jnp.bfloat16),
            pltpu.VMEM((rows, width), jnp.bfloat16),
            pltpu.SemaphoreType.DMA((2,)),
        ],
    )((place, left, right, weight_in, weight_out), after)


def hidden_kernel(pre_near, back_near, pre_sent, back_sent, weight, act, grad):
    pre_act = wide(pre_near[...]) + wide(pre_sent[...])
    back_grad = wide(back_near[...]) + wide(back_sent[...])
    activation, slopes = gelu_parts(pre_act)
    act[...] = low(activation * weight[...])
    grad[...] = low(back_grad * weight[...] * slopes)


def hidden(after, pre_near, back_near, pre_sent, back_sent, weight):
    rows, cols = pre_near.shape
    step = rows // 8
    spec = pl.BlockSpec((step, cols), lambda j: (j, 0))
    return call(
        hidden_kernel,
        [(rows, cols)] * 2,
        (rows // step,),
        [spec] * 4 + [pl.BlockSpec((step, 1), lambda j: (j, 0))],
        [spec] * 2,
        scalars=0,
    )((pre_near, back_near, pre_sent, back_sent, weight), after)


def input_kernel(n_chunks, steps, place, *refs):
    shares, weight, refs = refs[: 2 * n_chunks], refs[2 * n_chunks], refs[2 * n_chunks + 1 :]
    outs, (held, sems) = refs[:-2], refs[-2:]
    share, chunk = shares[0].shape
    step, each = pl.program_id(0), len(outs) // steps

    @pl.when(step == 0)
    def _():
        copies = []
        for i, ref in enumerate(shares):
            row = place[0] if i < n_chunks else 1 - place[0]
            rows = pl.ds(pl.multiple_of(row * share, share), share)
            copies.append(
                pltpu.make_async_copy(ref, held.at[rows, pl.ds((i % n_chunks) * chunk, chunk)], sems.at[i])
            )
        start_all(copies)

    part = low(contract_cols(held[...], weight[...]))
    if not each:
        outs[0][...] = part
        return
    cols = part.shape[1] // each
    for i in range(steps):

        @pl.when(step == i)
        def _(i=i):
            for k in range(each):
                outs[i * each + k][...] = part[:, k * cols : (k + 1) * cols]


def input_part(after, place, near, other, weight, first, pieces, each, cols):
    share, chunk = near[0].shape
    n_chunks = len(near)
    rows, width = 2 * share, chunk * n_chunks
    steps = pieces // each
    if pieces == 1:
        tile = cols // 6
        return call(
            functools.partial(input_kernel, n_chunks, 6),
            [(rows, cols)],
            (6,),
            [pl.BlockSpec(memory_space=pl.ANY)] * (2 * n_chunks)
            + [pl.BlockSpec((tile, width), lambda j, c: (j, 0))],
            [pl.BlockSpec((rows, tile), lambda j, c: (0, j))],
            [pltpu.VMEM((rows, width), jnp.bfloat16), pltpu.SemaphoreType.DMA((2 * n_chunks,))],
        )((place, *near, *other, weight), after)
    return call(
        functools.partial(input_kernel, n_chunks, steps),
        [(rows, cols)] * pieces,
        (steps,),
        [pl.BlockSpec(memory_space=pl.ANY)] * (2 * n_chunks)
        + [pl.BlockSpec((cols * each, width), lambda j, c: (first // each + j, 0))],
        [pl.BlockSpec((rows, cols), lambda j, c: (0, 0))] * pieces,
        [pltpu.VMEM((rows, width), jnp.bfloat16), pltpu.SemaphoreType.DMA((2 * n_chunks,))],
    )((place, *near, *other, weight), after)


def gather_hidden(offsets, place, shares, near, far, held, sides, sems):
    share, rows = shares[0].shape[0], near.shape[0]
    block, piece = sides.shape[1] // 2, far[0].shape[1]
    copies = []

    def add(source, target):
        copies.append(pltpu.make_async_copy(source, target, sems.at[len(copies)]))

    for i, ref in enumerate(shares):
        row = place[0] if i % 2 == 0 else 1 - place[0]
        row = pl.multiple_of((2 * (i // 2) + row) * share, share)
        add(ref, held.at[pl.ds(row, share)])
    for i, offset in enumerate(offsets):
        column = pl.multiple_of((place[1] ^ offset) * block, block)
        add(near.at[:, pl.ds(column, block)], sides.at[pl.ds(0, rows), pl.ds(i * block, block)])
    for i, ref in enumerate(far):
        add(ref, sides.at[pl.ds(rows, rows), pl.ds(i * piece, piece)])
    start_all(copies)


def grad_in_kernel(offsets, place, a, b, c, d, near, *refs):
    far, (sent, own, held, sides, sems) = refs[:-5], refs[-5:]
    step, tile = pl.program_id(0), sent.shape[1]
    block = sent.shape[0]

    @pl.when(step == 0)
    def _():
        gather_hidden(offsets, place, (a, b, c, d), near, far, held, sides, sems)

    cols = pl.ds(pl.multiple_of(step * tile, tile), tile)
    product = contract_rows(sides[...], held[:, cols])
    sent[...] = low(product[:block])
    own[...] = low(product[block:])


def grad_out_kernel(offsets, place, a, b, c, d, near, *refs):
    far, (sent, own, held, sides, sems) = refs[:-5], refs[-5:]
    step = pl.program_id(0)
    block = sent.shape[1]

    @pl.when(step == 0)
    def _():
        gather_hidden(offsets, place, (a, b, c, d), near, far, held, sides, sems)
        sent[...] = low(contract_rows(held[...], sides[:, :block]))

    @pl.when(step == 1)
    def _():
        own[...] = low(contract_rows(held[...], sides[:, block:]))


def weight_part(after, kernel, place, shares, near, far, offsets, block, tile):
    share, chunk = shares[0].shape
    if tile:
        outs, grid = (block, chunk), (chunk // tile,)
        out = pl.BlockSpec((block, tile), lambda j, c: (0, j))
    else:
        outs, grid = (chunk, block), (2,)
        out = pl.BlockSpec((chunk, block), lambda j, c: (0, 0))
    return call(
        functools.partial(kernel, offsets),
        [outs] * 2,
        grid,
        [pl.BlockSpec(memory_space=pl.ANY)] * (5 + len(far)),
        [out, out],
        [
            pltpu.VMEM((4 * share, chunk), jnp.bfloat16),
            pltpu.VMEM((4 * share, 2 * block), jnp.bfloat16),
            pltpu.SemaphoreType.DMA((6 + len(far),)),
        ],
    )((place, *shares, near, *far), after)


def line_kernel(jobs, *refs):
    at_end, refs = refs[0], list(refs[1:])
    ins = [refs.pop(0) for _ in range(2 * len(jobs))]
    if len(refs) > len(jobs):
        refs.pop(0)
    for i, job in enumerate(jobs):
        left, right = ins[2 * i][...], ins[2 * i + 1][...]
        if job == "last":
            refs[i][...] = jnp.where(at_end[0] == 1, right, left)
        else:
            refs[i][...] = low(wide(left) + wide(right))


def line_step(after, at_end, jobs, index, buffer, width):
    names = sorted(jobs)
    rows, cols = next(iter(jobs.values()))[0].shape
    step = rows // LINE_STEPS
    spec = pl.BlockSpec((step, cols), lambda j, c: (j, 0))
    outs, out_specs, args, aliases, in_specs = [], [], [at_end], {}, []
    for i, name in enumerate(names):
        args += jobs[name]
        in_specs += [spec, spec]
        if name == "last":
            outs.append((rows, width))
            out_specs.append(pl.BlockSpec((step, cols), lambda j, c: (j, index)))
        else:
            outs.append((rows, cols))
            out_specs.append(spec)
    if "last" in jobs and buffer is not None:
        aliases = {len(args): names.index("last")}
        args.append(buffer)
        in_specs.append(pl.BlockSpec(memory_space=pl.ANY))
    *results, mark = call(
        functools.partial(line_kernel, names), outs, (LINE_STEPS,), in_specs, out_specs, aliases=aliases
    )(args, after)
    return dict(zip(names, results)), mark


def sum_kernel(left, right, *refs):
    refs[-1][...] = low(wide(left[...]) + wide(right[...]))


def sum_into(after, left, right, buffer, shape, index, by_rows):
    rows, cols = left.shape
    steps = 4
    step = rows // steps
    spec = pl.BlockSpec((step, cols), lambda j: (j, 0))
    if by_rows:
        out = pl.BlockSpec((step, cols), lambda j: (index * steps + j, 0))
    else:
        out = pl.BlockSpec((step, cols), lambda j: (j, index))
    args, in_specs, aliases = [left, right], [spec, spec], {}
    if buffer is not None:
        args.append(buffer)
        in_specs.append(pl.BlockSpec(memory_space=pl.ANY))
        aliases = {2: 0}
    return call(sum_kernel, [shape], (steps,), in_specs, [out], scalars=0, aliases=aliases)(args, after)


def per_device(tokens, cotangent, weight_in, weight_out, segment_ids, keep_mask):
    sizes = tuple(lax.axis_size(axis) for axis in ("batch", "row", "col"))
    if sizes != (4, 2, 4) or weight_in.shape[1] % (FF_CHUNKS * 512) or tokens.shape[1] % (128 * PIECES):
        return per_device_any(tokens, cotangent, weight_in, weight_out, segment_ids, keep_mask)
    here, row, col = (lax.axis_index(axis) for axis in ("batch", "row", "col"))
    rows, width = tokens.shape
    hidden_cols = weight_in.shape[1]
    block, share, chunk = width // 4, rows // 2, hidden_cols // FF_CHUNKS
    place = jnp.stack([row, here]).astype(jnp.int32)
    at_end = ((col == 0) | (col == 3)).astype(jnp.int32).reshape(1)

    last = []

    def chain(run, *args, needs=()):
        *results, mark = run([*last, *needs], *args)
        last[:] = [mark]
        return results

    token_weight = image_weights(segment_ids, keep_mask)
    share_weight = lax.dynamic_slice_in_dim(token_weight, row * share, share)[:, None]
    last[:] = [token_weight]
    picked = chain(pick_columns, place, tokens, cotangent, (3, 1), (3, 2), block, PICKED, 256)
    tokens_far = [swap(x, "batch", 1) for x in picked[:PICKED]]
    cot_far = [swap(x, "batch", 2) for x in picked[PICKED:]]

    count = FF_CHUNKS
    partial, act_own, grad_own, act_other, grad_other = ([None] * count for _ in range(5))
    act_far, grad_far, act_swap, grad_swap = ([None] * count for _ in range(4))

    def forward(i, needs=()):
        own_pre, own_back, sent_pre, sent_back = chain(
            partial_products, place, tokens, cotangent, weight_in, weight_out, i, chunk, 512, needs=needs
        )
        partial[i] = (own_pre, own_back, swap(sent_pre, "row", 1), swap(sent_back, "row", 1))

    def activate(i, needs=()):
        act, grad = chain(hidden, *partial[i], share_weight, needs=needs)
        act_own[i], grad_own[i] = act, grad
        grad_other[i], act_other[i] = swap(grad, "row", 1), swap(act, "row", 1)
        grad_far[i], act_far[i] = swap(grad, "batch", 1), swap(act, "batch", 2)
        grad_swap[i], act_swap[i] = swap(grad_far[i], "row", 1), swap(act_far[i], "row", 1)

    cols = width // PIECES
    parts, inward = [], []
    half, across, total, outward = ([None] * PIECES for _ in range(4))
    grad_tokens = None

    def inputs(pieces, needs=()):
        made = chain(
            input_part, place, grad_own, grad_other, weight_in, len(parts), pieces, PIECE_CALL, cols, needs=needs
        )
        parts.extend(made)
        inward.extend(lax.ppermute(x, "col", [(0, 1), (3, 2)]) for x in made)

    def line(n, needs=()):
        nonlocal grad_tokens
        jobs = {}
        if n < PIECES:
            jobs["half"] = (parts[n], inward[n])
        if 0 <= n - 2 < PIECES:
            jobs["total"] = (half[n - 2], across[n - 2])
        if 0 <= n - 4 < PIECES:
            jobs["last"] = (total[n - 4], outward[n - 4])
        made, mark = line_step([*last, *needs], at_end, jobs, n - 4, grad_tokens, width)
        last[:] = [mark]
        if "half" in made:
            half[n] = made["half"]
            across[n] = lax.ppermute(half[n], "col", [(1, 2), (2, 1)])
        if "total" in made:
            total[n - 2] = made["total"]
            outward[n - 2] = lax.ppermute(total[n - 2], "col", [(1, 0), (2, 3)])
        grad_tokens = made.get("last", grad_tokens)

    in_own, out_own, in_sent, out_sent = ([None] * count for _ in range(4))

    def weights_in(i, needs=()):
        shares = (grad_own[i], grad_other[i], grad_far[i], grad_swap[i])
        sent, in_own[i] = chain(
            weight_part, grad_in_kernel, place, shares, tokens, tokens_far, (2, 0), block, 512, needs=needs
        )
        in_sent[i] = swap(sent, "batch", 2)

    def weights_out(i, needs=()):
        shares = (act_own[i], act_other[i], act_far[i], act_swap[i])
        sent, out_own[i] = chain(
            weight_part, grad_out_kernel, place, shares, cotangent, cot_far, (1, 0), block, 0, needs=needs
        )
        out_sent[i] = swap(sent, "batch", 1)

    grad_in = grad_out = None

    def finish(i):
        nonlocal grad_in, grad_out
        (grad_in,) = chain(sum_into, in_own[i], in_sent[i], grad_in, (block, hidden_cols), i, False)
        (grad_out,) = chain(sum_into, out_own[i], out_sent[i], grad_out, (hidden_cols, block), i, True)

    forward(0)
    forward(1)
    activate(0, needs=[*tokens_far, *cot_far])
    activate(1)
    (part,) = chain(input_part, place, grad_own, grad_other, weight_in, 0, 1, 1, width)
    grad_tokens = lax.psum(part, "col")
    weights_in(0, needs=[act_swap[0]])
    weights_out(0, needs=[grad_far[1], act_far[1]])
    weights_in(1)
    weights_out(1)
    finish(0)
    finish(1)
    return (grad_tokens, grad_in, grad_out)


def solution(mesh):
    return jax.shard_map(
        per_device,
        mesh=mesh,
        in_specs=(
            P("batch", "row"),
            P("batch", "row"),
            P("row", "col"),
            P("col", "row"),
            P("batch"),
            P("batch"),
        ),
        out_specs=(P("batch", "row"), P(("row", "batch"), "col"), P("col", ("row", "batch"))),
        check_vma=False,
    )
```

```python
import functools

import jax
import jax.numpy as jnp
from jax import lax
from jax.experimental import pallas as pl
from jax.experimental.pallas import tpu as pltpu
from jax.sharding import PartitionSpec as P

SEGS = 32
IMAGE_MEAN = 128
VMEM_BYTES = 60 * 2**20
FF_CHUNKS = 2
PIECES = 8
LINE_STEPS = 2
KERNEL_FLOPS = 10**6


inv_root_two = 0.7071067811865476
inv_root_tau = 0.3989422804014327


def padded(x, sides, width):
    for axis, dim in sides:
        size, length = (lax.axis_size(axis), x.shape[dim])
        up = [(i, (i + 1) % size) for i in range(size - 1)]
        down = [(j, i) for i, j in up]
        last = lax.slice_in_dim(x, length - width, length, axis=dim)
        first = lax.slice_in_dim(x, 0, width, axis=dim)
        before = lax.ppermute(last, axis, up)
        after = lax.ppermute(first, axis, down)
        x = jnp.concatenate([before, x, after], axis=dim)
    return x


def gelu_parts(pre_act):
    normal_cdf = 0.5 * (1.0 + lax.erf(pre_act * inv_root_two))
    slopes = normal_cdf + pre_act * jnp.exp(-0.5 * pre_act * pre_act) * inv_root_tau
    return (pre_act * normal_cdf, slopes)


def contract_cols(left, right):
    return lax.dot_general(
        left, right, (((1,), (1,)), ((), ())), preferred_element_type=jnp.float32
    )


def contract_rows(left, right):
    return lax.dot_general(
        left, right, (((0,), (0,)), ((), ())), preferred_element_type=jnp.float32
    )


def image_weights(segment_ids, keep_mask):
    labels = jnp.arange(SEGS, dtype=jnp.int32)
    onehot = (segment_ids[:, None] == labels[None, :]).astype(jnp.float32)
    keeping = keep_mask.astype(jnp.float32)
    local_sizes = jnp.sum(onehot * keeping[:, None], axis=0)
    beside = padded(local_sizes[None, :], (("batch", 0),), 1)
    image_sizes = jnp.sum(beside, axis=0)
    per_token = jnp.dot(onehot, image_sizes, precision=lax.Precision.HIGHEST)
    return keeping * jnp.sqrt(IMAGE_MEAN / jnp.maximum(per_token, 1.0))


def per_device_any(tokens, cotangent, weight_in, weight_out, segment_ids, keep_mask):
    token_weight = image_weights(segment_ids, keep_mask)
    scaled = (cotangent.astype(jnp.float32) * token_weight[:, None]).astype(jnp.bfloat16)
    hidden_cols = weight_in.shape[1]
    forward_rows = jnp.dot(tokens, weight_in, preferred_element_type=jnp.float32)
    backward_rows = contract_cols(scaled, weight_out)
    summed = lax.psum_scatter(
        jnp.concatenate([forward_rows, backward_rows], axis=1).astype(jnp.bfloat16),
        "row",
        scatter_dimension=0,
        tiled=True,
    ).astype(jnp.float32)
    act_share, slope_share = gelu_parts(summed[:, :hidden_cols])
    grad_share = (summed[:, hidden_cols:] * slope_share).astype(jnp.bfloat16)
    activation, hidden_grad = (
        lax.all_gather(act_share.astype(jnp.bfloat16), "row", axis=0, tiled=True),
        lax.all_gather(grad_share, "row", axis=0, tiled=True),
    )
    input_part = contract_cols(hidden_grad, weight_in)
    grad_tokens = lax.psum(input_part.astype(jnp.bfloat16), "col")
    first_grad = contract_rows(tokens, hidden_grad)
    second_grad = contract_rows(scaled, activation)
    summed_grads = lax.psum_scatter(
        jnp.concatenate([first_grad, second_grad], axis=1).astype(jnp.bfloat16),
        "batch",
        scatter_dimension=0,
        tiled=True,
    ).astype(jnp.float32)
    grad_in = summed_grads[:, :hidden_cols].astype(jnp.bfloat16)
    grad_out = summed_grads[:, hidden_cols:].T.astype(jnp.bfloat16)
    return (grad_tokens, grad_in, grad_out)


def low(x):
    return x.astype(jnp.bfloat16)


def wide(x):
    return x.astype(jnp.float32)


def swap(x, axis, mask):
    size = lax.axis_size(axis)
    return lax.ppermute(x, axis, [(i, i ^ mask) for i in range(size)])


def call(kernel, outs, grid, in_specs, out_specs, scratch=(), scalars=1, aliases=None):
    def run(args, after):
        first, waits, results = len(in_specs) + scalars, len(after), len(outs)

        def body(*refs):
            refs = refs[:first] + refs[first + waits :]
            kernel(*refs[: first + results], *refs[first + results + 1 :])

        anywhere = pl.BlockSpec(memory_space=pl.ANY)
        return pl.pallas_call(
            body,
            out_shape=[jax.ShapeDtypeStruct(shape, jnp.bfloat16) for shape in [*outs, (16, 128)]],
            grid_spec=pltpu.PrefetchScalarGridSpec(
                num_scalar_prefetch=scalars,
                grid=grid,
                in_specs=[*in_specs] + [anywhere] * waits,
                out_specs=[*out_specs, anywhere],
                scratch_shapes=list(scratch),
            ),
            input_output_aliases=aliases or {},
            compiler_params=pltpu.CompilerParams(vmem_limit_bytes=VMEM_BYTES, has_side_effects=True),
            cost_estimate=pl.CostEstimate(flops=KERNEL_FLOPS, bytes_accessed=0, transcendentals=0),
        )(*args, *after)

    return run


def start_all(copies):
    for copy in copies:
        copy.start()
    for copy in copies:
        copy.wait()


def release_kernel(*refs):
    pass


def release(after, *arrays):
    anywhere = pl.BlockSpec(memory_space=pl.ANY)
    count = len(arrays)
    return call(
        release_kernel,
        [x.shape for x in arrays],
        (1,),
        [anywhere] * count,
        [anywhere] * count,
        scalars=0,
        aliases={i: i for i in range(count)},
    )(arrays, after)


def picked_copies(place, held, pieces, offsets, sems):
    block = held.shape[1] // 4
    copies, start, column = [], 0, 0
    for piece in pieces:
        filled = 0
        while filled < piece.shape[1]:
            count = min(piece.shape[1] - filled, block - column % block)
            source = (place[1] ^ offsets[column // block]) * block + column % block
            copies.append(
                pltpu.make_async_copy(
                    held.at[:, pl.ds(pl.multiple_of(source, 128), count)],
                    piece.at[:, pl.ds(filled, count)],
                    sems.at[len(copies)],
                )
            )
            filled, column = filled + count, column + count
    return copies


def partial_kernel(steps, offsets, place, left, right, weight_in, weight_out, own_pre, own_back, sent_pre, *refs):
    sent_back, picked, (held_left, held_right, sems, pick_sems) = refs[0], refs[1:-4], refs[-4:]
    step = pl.program_id(0)
    share = own_pre.shape[0]
    copies = [
        pltpu.make_async_copy(left, held_left, sems.at[0]),
        pltpu.make_async_copy(right, held_right, sems.at[1]),
    ]
    pieces = len(picked) // 2
    picks = [
        picked_copies(place, held_left, picked[:pieces], offsets[0], pick_sems.at[0]),
        picked_copies(place, held_right, picked[pieces:], offsets[1], pick_sems.at[1]),
    ]

    def store(product, own, sent):
        mine = place[0] == 0
        own[...] = low(jnp.where(mine, product[:share], product[share:]))
        sent[...] = low(jnp.where(mine, product[share:], product[:share]))

    @pl.when(step == 0)
    def _():
        copies[0].start()
        copies[1].start()
        copies[0].wait()
        for copy in picks[0]:
            copy.start()

    @pl.when(step == steps)
    def _():
        copies[1].wait()
        for copy in picks[1]:
            copy.start()

    @pl.when(step < steps)
    def _():
        store(jnp.dot(held_left[...], weight_in[...], preferred_element_type=jnp.float32), own_pre, sent_pre)

    @pl.when(step >= steps)
    def _():
        store(contract_cols(held_right[...], weight_out[...]), own_back, sent_back)

    @pl.when(step == 2 * steps - 1)
    def _():
        for copy in picks[0] + picks[1]:
            copy.wait()


def partial_products(after, place, left, right, weight_in, weight_out, index, chunk, tile, offsets, widths):
    rows, width = left.shape
    steps = chunk // tile
    early = pl.BlockSpec((rows // 2, tile), lambda j, c: (0, jnp.minimum(j, steps - 1)))
    late = pl.BlockSpec((rows // 2, tile), lambda j, c: (0, jnp.maximum(j - steps, 0)))
    anywhere = pl.BlockSpec(memory_space=pl.ANY)
    return call(
        functools.partial(partial_kernel, steps, offsets),
        [(rows // 2, chunk)] * 4 + [(rows, count) for count in widths] * 2,
        (2 * steps,),
        [
            anywhere,
            anywhere,
            pl.BlockSpec((width, tile), lambda j, c: (0, index * steps + jnp.minimum(j, steps - 1))),
            pl.BlockSpec((tile, width), lambda j, c: (index * steps + jnp.maximum(j - steps, 0), 0)),
        ],
        [early, late, early, late] + [anywhere] * (2 * len(widths)),
        [
            pltpu.VMEM((rows, width), jnp.bfloat16),
            pltpu.VMEM((rows, width), jnp.bfloat16),
            pltpu.SemaphoreType.DMA((2,)),
            pltpu.SemaphoreType.DMA((2, 8)),
        ],
    )((place, left, right, weight_in, weight_out), after)


def hidden_kernel(pre_near, back_near, pre_sent, back_sent, weight, act, grad):
    pre_act = wide(pre_near[...]) + wide(pre_sent[...])
    back_grad = wide(back_near[...]) + wide(back_sent[...])
    activation, slopes = gelu_parts(pre_act)
    act[...] = low(activation * weight[...])
    grad[...] = low(back_grad * weight[...] * slopes)


def hidden(after, pre_near, back_near, pre_sent, back_sent, weight):
    rows, cols = pre_near.shape
    step = rows // 4
    spec = pl.BlockSpec((step, cols), lambda j: (j, 0))
    return call(
        hidden_kernel,
        [(rows, cols)] * 2,
        (rows // step,),
        [spec] * 4 + [pl.BlockSpec((step, 1), lambda j: (j, 0))],
        [spec] * 2,
        scalars=0,
    )((pre_near, back_near, pre_sent, back_sent, weight), after)


def input_kernel(n_chunks, steps, place, *refs):
    shares, weight, refs = refs[: 2 * n_chunks], refs[2 * n_chunks], refs[2 * n_chunks + 1 :]
    outs, (held, sems) = refs[:-2], refs[-2:]
    share, chunk = shares[0].shape
    step, each = pl.program_id(0), len(outs) // steps

    @pl.when(step == 0)
    def _():
        copies = []
        for i, ref in enumerate(shares):
            row = place[0] if i < n_chunks else 1 - place[0]
            rows = pl.ds(pl.multiple_of(row * share, share), share)
            copies.append(
                pltpu.make_async_copy(ref, held.at[rows, pl.ds((i % n_chunks) * chunk, chunk)], sems.at[i])
            )
        start_all(copies)

    part = low(contract_cols(held[...], weight[...]))
    if not each:
        outs[0][...] = part
        return
    cols = part.shape[1] // each
    for i in range(steps):

        @pl.when(step == i)
        def _(i=i):
            for k in range(each):
                outs[i * each + k][...] = part[:, k * cols : (k + 1) * cols]


def input_part(after, place, near, other, weight, first, pieces, each, cols):
    share, chunk = near[0].shape
    n_chunks = len(near)
    rows, width = 2 * share, chunk * n_chunks
    steps = pieces // each
    if pieces == 1:
        tile = 512
        return call(
            functools.partial(input_kernel, n_chunks, cols // tile),
            [(rows, cols)],
            (cols // tile,),
            [pl.BlockSpec(memory_space=pl.ANY)] * (2 * n_chunks)
            + [pl.BlockSpec((tile, width), lambda j, c: (j, 0))],
            [pl.BlockSpec((rows, tile), lambda j, c: (0, j))],
            [pltpu.VMEM((rows, width), jnp.bfloat16), pltpu.SemaphoreType.DMA((2 * n_chunks,))],
        )((place, *near, *other, weight), after)
    return call(
        functools.partial(input_kernel, n_chunks, steps),
        [(rows, cols)] * pieces,
        (steps,),
        [pl.BlockSpec(memory_space=pl.ANY)] * (2 * n_chunks)
        + [pl.BlockSpec((cols * each, width), lambda j, c: (first // each + j, 0))],
        [pl.BlockSpec((rows, cols), lambda j, c: (0, 0))] * pieces,
        [pltpu.VMEM((rows, width), jnp.bfloat16), pltpu.SemaphoreType.DMA((2 * n_chunks,))],
    )((place, *near, *other, weight), after)


def gather_hidden(offsets, place, shares, near, far, held, sides, sems):
    share, rows = shares[0].shape[0], near.shape[0]
    block = sides.shape[1] // 2
    copies = []

    def add(source, target):
        copies.append(pltpu.make_async_copy(source, target, sems.at[len(copies)]))

    for i, ref in enumerate(shares):
        row = place[0] if i % 2 == 0 else 1 - place[0]
        row = pl.multiple_of((2 * (i // 2) + row) * share, share)
        add(ref, held.at[pl.ds(row, share)])
    for i, offset in enumerate(offsets):
        column = pl.multiple_of((place[1] ^ offset) * block, block)
        add(near.at[:, pl.ds(column, block)], sides.at[pl.ds(0, rows), pl.ds(i * block, block)])
    column = 0
    for ref in far:
        add(ref, sides.at[pl.ds(rows, rows), pl.ds(column, ref.shape[1])])
        column += ref.shape[1]
    start_all(copies)


def grad_in_kernel(offsets, place, a, b, c, d, near, *refs):
    far, (sent, own, held, sides, sems) = refs[:-5], refs[-5:]
    step, tile = pl.program_id(0), sent.shape[1]
    block = sent.shape[0]

    @pl.when(step == 0)
    def _():
        gather_hidden(offsets, place, (a, b, c, d), near, far, held, sides, sems)

    cols = pl.ds(pl.multiple_of(step * tile, tile), tile)
    product = contract_rows(sides[...], held[:, cols])
    sent[...] = low(product[:block])
    own[...] = low(product[block:])


def grad_out_kernel(offsets, place, a, b, c, d, near, *refs):
    far, (sent, own, held, sides, sems) = refs[:-5], refs[-5:]
    step = pl.program_id(0)
    block = sent.shape[1]

    @pl.when(step == 0)
    def _():
        gather_hidden(offsets, place, (a, b, c, d), near, far, held, sides, sems)
        sent[...] = low(contract_rows(held[...], sides[:, :block]))

    @pl.when(step == 1)
    def _():
        own[...] = low(contract_rows(held[...], sides[:, block:]))


def weight_part(after, kernel, place, shares, near, far, offsets, block, tile):
    share, chunk = shares[0].shape
    if tile:
        outs, grid = (block, chunk), (chunk // tile,)
        out = pl.BlockSpec((block, tile), lambda j, c: (0, j))
    else:
        outs, grid = (chunk, block), (2,)
        out = pl.BlockSpec((chunk, block), lambda j, c: (0, 0))
    return call(
        functools.partial(kernel, offsets),
        [outs] * 2,
        grid,
        [pl.BlockSpec(memory_space=pl.ANY)] * (5 + len(far)),
        [out, out],
        [
            pltpu.VMEM((4 * share, chunk), jnp.bfloat16),
            pltpu.VMEM((4 * share, 2 * block), jnp.bfloat16),
            pltpu.SemaphoreType.DMA((6 + len(far),)),
        ],
    )((place, *shares, near, *far), after)


def line_kernel(jobs, *refs):
    at_end, refs = refs[0], list(refs[1:])
    ins = [refs.pop(0) for _ in range(2 * len(jobs))]
    if len(refs) > len(jobs):
        refs.pop(0)
    for i, job in enumerate(jobs):
        left, right = ins[2 * i][...], ins[2 * i + 1][...]
        if job == "last":
            refs[i][...] = jnp.where(at_end[0] == 1, right, left)
        else:
            refs[i][...] = low(wide(left) + wide(right))


def line_step(after, at_end, jobs, index, buffer, width):
    names = sorted(jobs)
    rows, cols = next(iter(jobs.values()))[0].shape
    step = rows // LINE_STEPS
    spec = pl.BlockSpec((step, cols), lambda j, c: (j, 0))
    outs, out_specs, args, aliases, in_specs = [], [], [at_end], {}, []
    for i, name in enumerate(names):
        args += jobs[name]
        in_specs += [spec, spec]
        if name == "last":
            outs.append((rows, width))
            out_specs.append(pl.BlockSpec((step, cols), lambda j, c: (j, index)))
        else:
            outs.append((rows, cols))
            out_specs.append(spec)
    if "last" in jobs and buffer is not None:
        aliases = {len(args): names.index("last")}
        args.append(buffer)
        in_specs.append(pl.BlockSpec(memory_space=pl.ANY))
    *results, mark = call(
        functools.partial(line_kernel, names), outs, (LINE_STEPS,), in_specs, out_specs, aliases=aliases
    )(args, after)
    return dict(zip(names, results)), mark


def sum_kernel(left, right, *refs):
    refs[-1][...] = low(wide(left[...]) + wide(right[...]))


def sum_into(after, left, right, buffer, shape, index, by_rows):
    rows, cols = left.shape
    steps = 4
    step = rows // steps
    spec = pl.BlockSpec((step, cols), lambda j: (j, 0))
    if by_rows:
        out = pl.BlockSpec((step, cols), lambda j: (index * steps + j, 0))
    else:
        out = pl.BlockSpec((step, cols), lambda j: (j, index))
    args, in_specs, aliases = [left, right], [spec, spec], {}
    if buffer is not None:
        args.append(buffer)
        in_specs.append(pl.BlockSpec(memory_space=pl.ANY))
        aliases = {2: 0}
    return call(sum_kernel, [shape], (steps,), in_specs, [out], scalars=0, aliases=aliases)(args, after)


def per_device(tokens, cotangent, weight_in, weight_out, segment_ids, keep_mask):
    sizes = tuple(lax.axis_size(axis) for axis in ("batch", "row", "col"))
    if sizes != (4, 2, 4) or weight_in.shape[1] % (FF_CHUNKS * 512) or tokens.shape[1] % (256 * PIECES // 2):
        return per_device_any(tokens, cotangent, weight_in, weight_out, segment_ids, keep_mask)
    here, row, col = (lax.axis_index(axis) for axis in ("batch", "row", "col"))
    rows, width = tokens.shape
    hidden_cols = weight_in.shape[1]
    block, share, chunk = width // 4, rows // 2, hidden_cols // FF_CHUNKS
    place = jnp.stack([row, here]).astype(jnp.int32)
    at_end = ((col == 0) | (col == 3)).astype(jnp.int32).reshape(1)

    last = []

    def chain(run, *args, needs=()):
        *results, mark = run([*last, *needs], *args)
        last[:] = [mark]
        return results

    token_weight = image_weights(segment_ids, keep_mask)
    share_weight = lax.dynamic_slice_in_dim(token_weight, row * share, share)[:, None]
    count = FF_CHUNKS
    partial, act_own, grad_own, act_other, grad_other = ([None] * count for _ in range(5))
    act_far, grad_far, act_swap, grad_swap = ([None] * count for _ in range(4))

    tokens_far, cot_far = [], []

    def forward(i, widths=(), needs=()):
        own_pre, own_back, sent_pre, sent_back, *picked = chain(
            partial_products,
            place,
            tokens,
            cotangent,
            weight_in,
            weight_out,
            i,
            chunk,
            512,
            ((3, 1), (3, 2)),
            widths,
            needs=needs,
        )
        partial[i] = (own_pre, own_back, swap(sent_pre, "row", 1), swap(sent_back, "row", 1))
        if picked:
            picked = chain(release, *picked, needs=[token_weight])
            tokens_far.extend(swap(x, "batch", 1) for x in picked[: len(widths)])
            cot_far.extend(swap(x, "batch", 2) for x in picked[len(widths) :])

    def activate(i, needs=()):
        act, grad = chain(hidden, *partial[i], share_weight, needs=needs)
        act_own[i], grad_own[i] = act, grad
        grad_other[i], act_other[i] = swap(grad, "row", 1), swap(act, "row", 1)
        grad_far[i], act_far[i] = swap(grad, "batch", 1), swap(act, "batch", 2)

    def exchange(i, needs=()):
        grad_far[i], act_far[i] = chain(release, grad_far[i], act_far[i], needs=needs)
        grad_swap[i], act_swap[i] = swap(grad_far[i], "row", 1), swap(act_far[i], "row", 1)

    cols = width // PIECES
    parts, inward = [], []
    half, across, total, outward = ([None] * PIECES for _ in range(4))
    grad_tokens = None

    def inputs(pieces, needs=()):
        made = chain(
            input_part, place, grad_own, grad_other, weight_in, len(parts), pieces, 2, cols, needs=needs
        )
        parts.extend(made)
        inward.extend(lax.ppermute(x, "col", [(0, 1), (3, 2)]) for x in made)

    def line(first=None, second=None, third=None, needs=()):
        nonlocal grad_tokens
        jobs = {}
        if first is not None:
            jobs["half"] = (parts[first], inward[first])
        if second is not None:
            jobs["total"] = (half[second], across[second])
        if third is not None:
            jobs["last"] = (total[third], outward[third])
        made, mark = line_step([*last, *needs], at_end, jobs, third, grad_tokens, width)
        last[:] = [mark]
        if first is not None:
            half[first] = made["half"]
            across[first] = lax.ppermute(half[first], "col", [(1, 2), (2, 1)])
        if second is not None:
            total[second] = made["total"]
            outward[second] = lax.ppermute(total[second], "col", [(1, 0), (2, 3)])
        grad_tokens = made.get("last", grad_tokens)

    in_own, out_own, in_sent, out_sent = ([None] * count for _ in range(4))

    def weights_in(i, needs=()):
        shares = (grad_own[i], grad_other[i], grad_far[i], grad_swap[i])
        sent, in_own[i] = chain(
            weight_part, grad_in_kernel, place, shares, tokens, tokens_far, (2, 0), block, 512, needs=needs
        )
        in_sent[i] = swap(sent, "batch", 2)

    def weights_out(i, needs=()):
        shares = (act_own[i], act_other[i], act_far[i], act_swap[i])
        sent, out_own[i] = chain(
            weight_part, grad_out_kernel, place, shares, cotangent, cot_far, (1, 0), block, 0, needs=needs
        )
        out_sent[i] = swap(sent, "batch", 1)

    grad_in = grad_out = None

    def finish(i):
        nonlocal grad_in, grad_out
        (grad_in,) = chain(sum_into, in_own[i], in_sent[i], grad_in, (block, hidden_cols), i, False)
        (grad_out,) = chain(sum_into, out_own[i], out_sent[i], grad_out, (hidden_cols, block), i, True)

    early = (2 * block * 7 // 12) // 128 * 128
    forward(0, (early, 2 * block - early))
    forward(1)
    activate(0)
    activate(1, needs=[tokens_far[0], cot_far[0]])
    (part,) = chain(input_part, place, grad_own, grad_other, weight_in, 0, 1, 1, width)
    grad_tokens = lax.psum(part, "col")
    exchange(0, needs=[tokens_far[1], cot_far[1]])
    weights_in(0)
    weights_out(0)
    exchange(1)
    weights_in(1)
    weights_out(1)
    finish(0)
    finish(1)
    return (grad_tokens, grad_in, grad_out)


def solution(mesh):
    return jax.shard_map(
        per_device,
        mesh=mesh,
        in_specs=(
            P("batch", "row"),
            P("batch", "row"),
            P("row", "col"),
            P("col", "row"),
            P("batch"),
            P("batch"),
        ),
        out_specs=(P("batch", "row"), P(("row", "batch"), "col"), P("col", ("row", "batch"))),
        check_vma=False,
    )
```

```python
import functools

import jax
import jax.numpy as jnp
from jax import lax
from jax.experimental import pallas as pl
from jax.experimental.pallas import tpu as pltpu
from jax.sharding import PartitionSpec as P

SEGS = 32
IMAGE_MEAN = 128
VMEM_BYTES = 60 * 2**20
PIECES = 8
LINE_STEPS = 2
KERNEL_FLOPS = 10**6


inv_root_two = 0.7071067811865476
inv_root_tau = 0.3989422804014327


def padded(x, sides, width):
    for axis, dim in sides:
        size, length = (lax.axis_size(axis), x.shape[dim])
        up = [(i, (i + 1) % size) for i in range(size - 1)]
        down = [(j, i) for i, j in up]
        last = lax.slice_in_dim(x, length - width, length, axis=dim)
        first = lax.slice_in_dim(x, 0, width, axis=dim)
        before = lax.ppermute(last, axis, up)
        after = lax.ppermute(first, axis, down)
        x = jnp.concatenate([before, x, after], axis=dim)
    return x


def gelu_parts(pre_act):
    normal_cdf = 0.5 * (1.0 + lax.erf(pre_act * inv_root_two))
    slopes = normal_cdf + pre_act * jnp.exp(-0.5 * pre_act * pre_act) * inv_root_tau
    return (pre_act * normal_cdf, slopes)


def contract_cols(left, right):
    return lax.dot_general(
        left, right, (((1,), (1,)), ((), ())), preferred_element_type=jnp.float32
    )


def contract_rows(left, right):
    return lax.dot_general(
        left, right, (((0,), (0,)), ((), ())), preferred_element_type=jnp.float32
    )


def image_counts(segment_ids, keep_mask):
    labels = jnp.arange(SEGS, dtype=jnp.int32)
    onehot = (segment_ids[:, None] == labels[None, :]).astype(jnp.float32)
    return jnp.sum(onehot * keep_mask.astype(jnp.float32)[:, None], axis=0)


def image_weights(segment_ids, keep_mask, image_sizes):
    labels = jnp.arange(SEGS, dtype=jnp.int32)
    onehot = (segment_ids[:, None] == labels[None, :]).astype(jnp.float32)
    per_token = jnp.dot(onehot, image_sizes, precision=lax.Precision.HIGHEST)
    return keep_mask.astype(jnp.float32) * jnp.sqrt(IMAGE_MEAN / jnp.maximum(per_token, 1.0))


def per_device_any(tokens, cotangent, weight_in, weight_out, segment_ids, keep_mask):
    local_sizes = image_counts(segment_ids, keep_mask)
    beside = padded(local_sizes[None, :], (("batch", 0),), 1)
    image_sizes = jnp.sum(beside, axis=0)
    token_weight = image_weights(segment_ids, keep_mask, image_sizes)
    scaled = (cotangent.astype(jnp.float32) * token_weight[:, None]).astype(jnp.bfloat16)
    hidden_cols = weight_in.shape[1]
    forward_rows = jnp.dot(tokens, weight_in, preferred_element_type=jnp.float32)
    backward_rows = contract_cols(scaled, weight_out)
    summed = lax.psum_scatter(
        jnp.concatenate([forward_rows, backward_rows], axis=1).astype(jnp.bfloat16),
        "row",
        scatter_dimension=0,
        tiled=True,
    ).astype(jnp.float32)
    act_share, slope_share = gelu_parts(summed[:, :hidden_cols])
    grad_share = (summed[:, hidden_cols:] * slope_share).astype(jnp.bfloat16)
    activation, hidden_grad = (
        lax.all_gather(act_share.astype(jnp.bfloat16), "row", axis=0, tiled=True),
        lax.all_gather(grad_share, "row", axis=0, tiled=True),
    )
    input_part = contract_cols(hidden_grad, weight_in)
    grad_tokens = lax.psum(input_part.astype(jnp.bfloat16), "col")
    first_grad = contract_rows(tokens, hidden_grad)
    second_grad = contract_rows(scaled, activation)
    summed_grads = lax.psum_scatter(
        jnp.concatenate([first_grad, second_grad], axis=1).astype(jnp.bfloat16),
        "batch",
        scatter_dimension=0,
        tiled=True,
    ).astype(jnp.float32)
    grad_in = summed_grads[:, :hidden_cols].astype(jnp.bfloat16)
    grad_out = summed_grads[:, hidden_cols:].T.astype(jnp.bfloat16)
    return (grad_tokens, grad_in, grad_out)


def low(x):
    return x.astype(jnp.bfloat16)


def wide(x):
    return x.astype(jnp.float32)


def swap(x, axis, mask):
    size = lax.axis_size(axis)
    return lax.ppermute(x, axis, [(i, i ^ mask) for i in range(size)])


def call(kernel, outs, grid, in_specs, out_specs, scratch=(), scalars=1, aliases=None):
    def run(args, after):
        first, waits, results = len(in_specs) + scalars, len(after), len(outs)

        def body(*refs):
            refs = refs[:first] + refs[first + waits :]
            kernel(*refs[: first + results], *refs[first + results + 1 :])

        anywhere = pl.BlockSpec(memory_space=pl.ANY)
        return pl.pallas_call(
            body,
            out_shape=[jax.ShapeDtypeStruct(shape, jnp.bfloat16) for shape in [*outs, (16, 128)]],
            grid_spec=pltpu.PrefetchScalarGridSpec(
                num_scalar_prefetch=scalars,
                grid=grid,
                in_specs=[*in_specs] + [anywhere] * waits,
                out_specs=[*out_specs, anywhere],
                scratch_shapes=list(scratch),
            ),
            input_output_aliases=aliases or {},
            compiler_params=pltpu.CompilerParams(vmem_limit_bytes=VMEM_BYTES, has_side_effects=True),
            cost_estimate=pl.CostEstimate(flops=KERNEL_FLOPS, bytes_accessed=0, transcendentals=0),
        )(*args, *after)

    return run


def start_all(copies):
    for copy in copies:
        copy.start()
    for copy in copies:
        copy.wait()


def release_kernel(*refs):
    pass


def release(after, *arrays):
    anywhere = pl.BlockSpec(memory_space=pl.ANY)
    count = len(arrays)
    return call(
        release_kernel,
        [x.shape for x in arrays],
        (1,),
        [anywhere] * count,
        [anywhere] * count,
        scalars=0,
        aliases={i: i for i in range(count)},
    )(arrays, after)


def picked_copies(place, held, pieces, offsets, sems):
    block = held.shape[1] // 4
    copies, start, column = [], 0, 0
    for piece in pieces:
        filled = 0
        while filled < piece.shape[1]:
            count = min(piece.shape[1] - filled, block - column % block)
            source = (place[1] ^ offsets[column // block]) * block + column % block
            copies.append(
                pltpu.make_async_copy(
                    held.at[:, pl.ds(pl.multiple_of(source, 128), count)],
                    piece.at[:, pl.ds(filled, count)],
                    sems.at[len(copies)],
                )
            )
            filled, column = filled + count, column + count
    return copies


def partial_kernel(steps, offsets, place, left, right, weight_in, weight_out, own_pre, own_back, sent_pre, *refs):
    sent_back, picked, (held_left, held_right, sems, pick_sems) = refs[0], refs[1:-4], refs[-4:]
    step = pl.program_id(0)
    share = own_pre.shape[0]
    copies = [
        pltpu.make_async_copy(left, held_left, sems.at[0]),
        pltpu.make_async_copy(right, held_right, sems.at[1]),
    ]
    pieces = len(picked) // 2
    picks = [
        picked_copies(place, held_left, picked[:pieces], offsets[0], pick_sems.at[0]),
        picked_copies(place, held_right, picked[pieces:], offsets[1], pick_sems.at[1]),
    ]

    def store(product, own, sent):
        mine = place[0] == 0
        own[...] = low(jnp.where(mine, product[:share], product[share:]))
        sent[...] = low(jnp.where(mine, product[share:], product[:share]))

    @pl.when(step == 0)
    def _():
        copies[0].start()
        copies[1].start()
        copies[0].wait()
        for copy in picks[0]:
            copy.start()

    @pl.when(step == steps)
    def _():
        copies[1].wait()
        for copy in picks[1]:
            copy.start()

    @pl.when(step < steps)
    def _():
        store(jnp.dot(held_left[...], weight_in[...], preferred_element_type=jnp.float32), own_pre, sent_pre)

    @pl.when(step >= steps)
    def _():
        store(contract_cols(held_right[...], weight_out[...]), own_back, sent_back)

    @pl.when(step == 2 * steps - 1)
    def _():
        for copy in picks[0] + picks[1]:
            copy.wait()


def partial_products(after, place, left, right, weight_in, weight_out, first, chunk, tile, offsets, widths):
    rows, width = left.shape
    steps, base = chunk // tile, first // tile
    early = pl.BlockSpec((rows // 2, tile), lambda j, c: (0, jnp.minimum(j, steps - 1)))
    late = pl.BlockSpec((rows // 2, tile), lambda j, c: (0, jnp.maximum(j - steps, 0)))
    anywhere = pl.BlockSpec(memory_space=pl.ANY)
    return call(
        functools.partial(partial_kernel, steps, offsets),
        [(rows // 2, chunk)] * 4 + [(rows, count) for count in widths] * 2,
        (2 * steps,),
        [
            anywhere,
            anywhere,
            pl.BlockSpec((width, tile), lambda j, c: (0, base + jnp.minimum(j, steps - 1))),
            pl.BlockSpec((tile, width), lambda j, c: (base + jnp.maximum(j - steps, 0), 0)),
        ],
        [early, late, early, late] + [anywhere] * (2 * len(widths)),
        [
            pltpu.VMEM((rows, width), jnp.bfloat16),
            pltpu.VMEM((rows, width), jnp.bfloat16),
            pltpu.SemaphoreType.DMA((2,)),
            pltpu.SemaphoreType.DMA((2, 8)),
        ],
    )((place, left, right, weight_in, weight_out), after)


def hidden_kernel(pre_near, back_near, pre_sent, back_sent, act, grad):
    pre_act = wide(pre_near[...]) + wide(pre_sent[...])
    back_grad = wide(back_near[...]) + wide(back_sent[...])
    activation, slopes = gelu_parts(pre_act)
    act[...] = low(activation)
    grad[...] = low(back_grad * slopes)


def hidden(after, pre_near, back_near, pre_sent, back_sent):
    rows, cols = pre_near.shape
    step = rows // 4
    spec = pl.BlockSpec((step, cols), lambda j: (j, 0))
    return call(
        hidden_kernel,
        [(rows, cols)] * 2,
        (rows // step,),
        [spec] * 4,
        [spec] * 2,
        scalars=0,
    )((pre_near, back_near, pre_sent, back_sent), after)


def input_kernel(n_chunks, steps, place, *refs):
    shares, weight, refs = refs[: 2 * n_chunks], refs[2 * n_chunks], refs[2 * n_chunks + 1 :]
    outs, (held, sems) = refs[:-2], refs[-2:]
    share = shares[0].shape[0]
    firsts = [sum(ref.shape[1] for ref in shares[:i]) for i in range(n_chunks)]
    step, each = pl.program_id(0), len(outs) // steps

    @pl.when(step == 0)
    def _():
        copies = []
        for i, ref in enumerate(shares):
            row = place[0] if i < n_chunks else 1 - place[0]
            rows = pl.ds(pl.multiple_of(row * share, share), share)
            cols = pl.ds(firsts[i % n_chunks], ref.shape[1])
            copies.append(pltpu.make_async_copy(ref, held.at[rows, cols], sems.at[i]))
        start_all(copies)

    part = low(contract_cols(held[...], weight[...]))
    if not each:
        outs[0][...] = part
        return
    cols = part.shape[1] // each
    for i in range(steps):

        @pl.when(step == i)
        def _(i=i):
            for k in range(each):
                outs[i * each + k][...] = part[:, k * cols : (k + 1) * cols]


def input_part(after, place, near, other, weight, first, pieces, each, cols):
    share = near[0].shape[0]
    n_chunks = len(near)
    rows, width = 2 * share, sum(x.shape[1] for x in near)
    steps = pieces // each
    if pieces == 1:
        tile = 512
        return call(
            functools.partial(input_kernel, n_chunks, cols // tile),
            [(rows, cols)],
            (cols // tile,),
            [pl.BlockSpec(memory_space=pl.ANY)] * (2 * n_chunks)
            + [pl.BlockSpec((tile, width), lambda j, c: (j, 0))],
            [pl.BlockSpec((rows, tile), lambda j, c: (0, j))],
            [pltpu.VMEM((rows, width), jnp.bfloat16), pltpu.SemaphoreType.DMA((2 * n_chunks,))],
        )((place, *near, *other, weight), after)
    return call(
        functools.partial(input_kernel, n_chunks, steps),
        [(rows, cols)] * pieces,
        (steps,),
        [pl.BlockSpec(memory_space=pl.ANY)] * (2 * n_chunks)
        + [pl.BlockSpec((cols * each, width), lambda j, c: (first // each + j, 0))],
        [pl.BlockSpec((rows, cols), lambda j, c: (0, 0))] * pieces,
        [pltpu.VMEM((rows, width), jnp.bfloat16), pltpu.SemaphoreType.DMA((2 * n_chunks,))],
    )((place, *near, *other, weight), after)


def gather_hidden(offsets, first, place, shares, near, far, held, sides, sems):
    share, rows = shares[0].shape[0], near.shape[0]
    block = sides.shape[1] // 2
    copies = []

    def add(source, target):
        copies.append(pltpu.make_async_copy(source, target, sems.at[len(copies)]))

    for i, ref in enumerate(shares):
        row = place[0] if i % 2 == 0 else 1 - place[0]
        row = pl.multiple_of((2 * (i // 2) + row) * share, share)
        add(ref.at[:, pl.ds(first, held.shape[1])], held.at[pl.ds(row, share)])
    for i, offset in enumerate(offsets):
        column = pl.multiple_of((place[1] ^ offset) * block, block)
        add(near.at[:, pl.ds(column, block)], sides.at[pl.ds(0, rows), pl.ds(i * block, block)])
    column = 0
    for ref in far:
        add(ref, sides.at[pl.ds(rows, rows), pl.ds(column, ref.shape[1])])
        column += ref.shape[1]
    start_all(copies)


def weigh(sides, weight):
    step = 256

    def body(i, carry):
        rows = pl.ds(pl.multiple_of(i * step, step), step)
        sides[rows, :] = low(wide(sides[rows, :]) * weight[rows, :])
        return carry

    lax.fori_loop(0, sides.shape[0] // step, body, 0)


def grad_in_kernel(offsets, first, place, a, b, c, d, near, weight, *refs):
    far, (sent, own, held, sides, sems) = refs[:-5], refs[-5:]
    step, tile = pl.program_id(0), sent.shape[1]
    block = sent.shape[0]

    @pl.when(step == 0)
    def _():
        gather_hidden(offsets, first, place, (a, b, c, d), near, far, held, sides, sems)
        weigh(sides, weight)

    cols = pl.ds(pl.multiple_of(step * tile, tile), tile)
    product = contract_rows(sides[...], held[:, cols])
    sent[...] = low(product[:block])
    own[...] = low(product[block:])


def grad_out_kernel(offsets, first, place, a, b, c, d, near, weight, *refs):
    far, (sent, own, held, sides, sems) = refs[:-5], refs[-5:]
    step = pl.program_id(0)
    block = sent.shape[1]

    @pl.when(step == 0)
    def _():
        gather_hidden(offsets, first, place, (a, b, c, d), near, far, held, sides, sems)
        weigh(sides, weight)
        sent[...] = low(contract_rows(held[...], sides[:, :block]))

    @pl.when(step == 1)
    def _():
        own[...] = low(contract_rows(held[...], sides[:, block:]))


def weight_part(after, kernel, place, shares, near, far, weight, offsets, first, chunk, block, tile):
    share = shares[0].shape[0]
    if tile:
        outs, grid = (block, chunk), (chunk // tile,)
        out = pl.BlockSpec((block, tile), lambda j, c: (0, j))
    else:
        outs, grid = (chunk, block), (2,)
        out = pl.BlockSpec((chunk, block), lambda j, c: (0, 0))
    return call(
        functools.partial(kernel, offsets, first),
        [outs] * 2,
        grid,
        [pl.BlockSpec(memory_space=pl.ANY)] * 5
        + [pl.BlockSpec(weight.shape, lambda j, c: (0, 0))]
        + [pl.BlockSpec(memory_space=pl.ANY)] * len(far),
        [out, out],
        [
            pltpu.VMEM((4 * share, chunk), jnp.bfloat16),
            pltpu.VMEM((4 * share, 2 * block), jnp.bfloat16),
            pltpu.SemaphoreType.DMA((6 + len(far),)),
        ],
    )((place, *shares, near, weight, *far), after)


def line_kernel(jobs, *refs):
    at_end, refs = refs[0], list(refs[1:])
    ins = [refs.pop(0) for _ in range(2 * len(jobs))]
    if len(refs) > len(jobs):
        refs.pop(0)
    for i, job in enumerate(jobs):
        left, right = ins[2 * i][...], ins[2 * i + 1][...]
        if job == "last":
            refs[i][...] = jnp.where(at_end[0] == 1, right, left)
        else:
            refs[i][...] = low(wide(left) + wide(right))


def line_step(after, at_end, jobs, index, buffer, width):
    names = sorted(jobs)
    rows, cols = next(iter(jobs.values()))[0].shape
    step = rows // LINE_STEPS
    spec = pl.BlockSpec((step, cols), lambda j, c: (j, 0))
    outs, out_specs, args, aliases, in_specs = [], [], [at_end], {}, []
    for i, name in enumerate(names):
        args += jobs[name]
        in_specs += [spec, spec]
        if name == "last":
            outs.append((rows, width))
            out_specs.append(pl.BlockSpec((step, cols), lambda j, c: (j, index)))
        else:
            outs.append((rows, cols))
            out_specs.append(spec)
    if "last" in jobs and buffer is not None:
        aliases = {len(args): names.index("last")}
        args.append(buffer)
        in_specs.append(pl.BlockSpec(memory_space=pl.ANY))
    *results, mark = call(
        functools.partial(line_kernel, names), outs, (LINE_STEPS,), in_specs, out_specs, aliases=aliases
    )(args, after)
    return dict(zip(names, results)), mark


def sum_kernel(left, right, *refs):
    refs[-1][...] = low(wide(left[...]) + wide(right[...]))


def sum_into(after, left, right, buffer, shape, index, by_rows):
    rows, cols = left.shape
    steps = 4
    step = rows // steps
    spec = pl.BlockSpec((step, cols), lambda j: (j, 0))
    if by_rows:
        out = pl.BlockSpec((step, cols), lambda j: (index * steps + j, 0))
    else:
        out = pl.BlockSpec((step, cols), lambda j: (j, index))
    args, in_specs, aliases = [left, right], [spec, spec], {}
    if buffer is not None:
        args.append(buffer)
        in_specs.append(pl.BlockSpec(memory_space=pl.ANY))
        aliases = {2: 0}
    return call(sum_kernel, [shape], (steps,), in_specs, [out], scalars=0, aliases=aliases)(args, after)


def per_device(tokens, cotangent, weight_in, weight_out, segment_ids, keep_mask):
    sizes = tuple(lax.axis_size(axis) for axis in ("batch", "row", "col"))
    if sizes != (4, 2, 4) or weight_in.shape[1] % 1536 or tokens.shape[1] % (256 * PIECES // 2):
        return per_device_any(tokens, cotangent, weight_in, weight_out, segment_ids, keep_mask)
    here, row, col = (lax.axis_index(axis) for axis in ("batch", "row", "col"))
    rows, width = tokens.shape
    hidden_cols = weight_in.shape[1]
    block, share = width // 4, rows // 2
    chunks = (hidden_cols // 3 * 2, hidden_cols // 3)
    firsts = (0, chunks[0])
    place = jnp.stack([row, here]).astype(jnp.int32)
    at_end = ((col == 0) | (col == 3)).astype(jnp.int32).reshape(1)

    last = []

    def chain(run, *args, needs=()):
        *results, mark = run([*last, *needs], *args)
        last[:] = [mark]
        return results

    marks = jnp.stack([segment_ids, keep_mask])
    marks = [marks] + [swap(marks, "batch", mask) for mask in (1, 2, 3)]
    image_sizes = sum(image_counts(*pair) for pair in marks)
    token_weight, weight_x, weight_y = (image_weights(*pair, image_sizes)[:, None] for pair in marks[:3])
    weight_in_pair = jnp.concatenate([token_weight, weight_x], axis=0)
    weight_out_pair = jnp.concatenate([token_weight, weight_y], axis=0)
    count = len(chunks)
    partial, act_own, grad_own, act_other, grad_other = ([None] * count for _ in range(5))
    act_far, grad_far, act_swap, grad_swap = ([None] * count for _ in range(4))

    tokens_far, cot_far = [], []

    def forward(i, widths=(), needs=()):
        own_pre, own_back, sent_pre, sent_back, *picked = chain(
            partial_products,
            place,
            tokens,
            cotangent,
            weight_in,
            weight_out,
            firsts[i],
            chunks[i],
            512,
            ((3, 1), (3, 2)),
            widths,
            needs=needs,
        )
        partial[i] = (own_pre, own_back, swap(sent_pre, "row", 1), swap(sent_back, "row", 1))
        if picked:
            tokens_far.extend(swap(x, "batch", 1) for x in picked[: len(widths)])
            cot_far.extend(swap(x, "batch", 2) for x in picked[len(widths) :])

    def activate(i, needs=()):
        act, grad = chain(hidden, *partial[i], needs=needs)
        act_own[i], grad_own[i] = act, grad
        grad_other[i], act_other[i] = swap(grad, "row", 1), swap(act, "row", 1)
        grad_far[i], act_far[i] = swap(grad, "batch", 1), swap(act, "batch", 2)

    def exchange(i, needs=()):
        grad_far[i], act_far[i] = chain(release, grad_far[i], act_far[i], needs=needs)
        grad_swap[i], act_swap[i] = swap(grad_far[i], "row", 1), swap(act_far[i], "row", 1)

    cols = width // PIECES
    parts, inward = [], []
    half, across, total, outward = ([None] * PIECES for _ in range(4))
    grad_tokens = None

    def inputs(pieces, needs=()):
        made = chain(
            input_part, place, grad_own, grad_other, weight_in, len(parts), pieces, 2, cols, needs=needs
        )
        parts.extend(made)
        inward.extend(lax.ppermute(x, "col", [(0, 1), (3, 2)]) for x in made)

    def line(first=None, second=None, third=None, needs=()):
        nonlocal grad_tokens
        jobs = {}
        if first is not None:
            jobs["half"] = (parts[first], inward[first])
        if second is not None:
            jobs["total"] = (half[second], across[second])
        if third is not None:
            jobs["last"] = (total[third], outward[third])
        made, mark = line_step([*last, *needs], at_end, jobs, third, grad_tokens, width)
        last[:] = [mark]
        if first is not None:
            half[first] = made["half"]
            across[first] = lax.ppermute(half[first], "col", [(1, 2), (2, 1)])
        if second is not None:
            total[second] = made["total"]
            outward[second] = lax.ppermute(total[second], "col", [(1, 0), (2, 3)])
        grad_tokens = made.get("last", grad_tokens)

    part = chunks[-1]
    places = [(i, k) for i in range(count) for k in range(chunks[i] // part)]
    in_own, out_own, in_sent, out_sent = ([None] * len(places) for _ in range(4))

    def weights_in(n, needs=()):
        i, k = places[n]
        shares = (grad_own[i], grad_other[i], grad_far[i], grad_swap[i])
        sent, in_own[n] = chain(
            weight_part, grad_in_kernel, place, shares, tokens, tokens_far, weight_in_pair, (2, 0), k * part, part, block, 512, needs=needs
        )
        in_sent[n] = swap(sent, "batch", 2)

    def weights_out(n, needs=()):
        i, k = places[n]
        shares = (act_own[i], act_other[i], act_far[i], act_swap[i])
        sent, out_own[n] = chain(
            weight_part, grad_out_kernel, place, shares, cotangent, cot_far, weight_out_pair, (1, 0), k * part, part, block, 0, needs=needs
        )
        out_sent[n] = swap(sent, "batch", 1)

    grad_in = grad_out = None

    def finish(i):
        nonlocal grad_in, grad_out
        (grad_in,) = chain(sum_into, in_own[i], in_sent[i], grad_in, (block, hidden_cols), i, False)
        (grad_out,) = chain(sum_into, out_own[i], out_sent[i], grad_out, (hidden_cols, block), i, True)

    early = (2 * block * 5 // 12) // 128 * 128
    forward(0, (early, 2 * block - early))
    forward(1)
    activate(0)
    activate(1, needs=[tokens_far[0], cot_far[0]])
    (summand,) = chain(input_part, place, grad_own, grad_other, weight_in, 0, 1, 1, width)
    grad_tokens = low(wide(lax.psum(summand, "col")) * token_weight)
    exchange(0, needs=[tokens_far[1], cot_far[1], weight_in_pair, weight_out_pair])
    weights_in(0)
    weights_out(0)
    weights_in(1)
    exchange(1)
    weights_out(1)
    weights_in(2)
    weights_out(2)
    finish(0)
    finish(1)
    finish(2)
    return (grad_tokens, grad_in, grad_out)


def solution(mesh):
    return jax.shard_map(
        per_device,
        mesh=mesh,
        in_specs=(
            P("batch", "row"),
            P("batch", "row"),
            P("row", "col"),
            P("col", "row"),
            P("batch"),
            P("batch"),
        ),
        out_specs=(P("batch", "row"), P(("row", "batch"), "col"), P("col", ("row", "batch"))),
        check_vma=False,
    )
```

```python
import functools

import jax
import jax.numpy as jnp
from jax import lax
from jax.experimental import pallas as pl
from jax.experimental.pallas import tpu as pltpu
from jax.sharding import PartitionSpec as P

SEGS = 32
IMAGE_MEAN = 128
VMEM_BYTES = 60 * 2**20
PIECES = 8
LINE_STEPS = 2
KERNEL_FLOPS = 10**6


inv_root_two = 0.7071067811865476
inv_root_tau = 0.3989422804014327


def padded(x, sides, width):
    for axis, dim in sides:
        size, length = (lax.axis_size(axis), x.shape[dim])
        up = [(i, (i + 1) % size) for i in range(size - 1)]
        down = [(j, i) for i, j in up]
        last = lax.slice_in_dim(x, length - width, length, axis=dim)
        first = lax.slice_in_dim(x, 0, width, axis=dim)
        before = lax.ppermute(last, axis, up)
        after = lax.ppermute(first, axis, down)
        x = jnp.concatenate([before, x, after], axis=dim)
    return x


def gelu_parts(pre_act):
    normal_cdf = 0.5 * (1.0 + lax.erf(pre_act * inv_root_two))
    slopes = normal_cdf + pre_act * jnp.exp(-0.5 * pre_act * pre_act) * inv_root_tau
    return (pre_act * normal_cdf, slopes)


def contract_cols(left, right):
    return lax.dot_general(
        left, right, (((1,), (1,)), ((), ())), preferred_element_type=jnp.float32
    )


def contract_rows(left, right):
    return lax.dot_general(
        left, right, (((0,), (0,)), ((), ())), preferred_element_type=jnp.float32
    )


def image_counts(segment_ids, keep_mask):
    labels = jnp.arange(SEGS, dtype=jnp.int32)
    onehot = (segment_ids[:, None] == labels[None, :]).astype(jnp.float32)
    return jnp.sum(onehot * keep_mask.astype(jnp.float32)[:, None], axis=0)


def image_weights(segment_ids, keep_mask, image_sizes):
    labels = jnp.arange(SEGS, dtype=jnp.int32)
    onehot = (segment_ids[:, None] == labels[None, :]).astype(jnp.float32)
    per_token = jnp.dot(onehot, image_sizes, precision=lax.Precision.HIGHEST)
    return keep_mask.astype(jnp.float32) * jnp.sqrt(IMAGE_MEAN / jnp.maximum(per_token, 1.0))


def per_device_any(tokens, cotangent, weight_in, weight_out, segment_ids, keep_mask):
    local_sizes = image_counts(segment_ids, keep_mask)
    beside = padded(local_sizes[None, :], (("batch", 0),), 1)
    image_sizes = jnp.sum(beside, axis=0)
    token_weight = image_weights(segment_ids, keep_mask, image_sizes)
    scaled = (cotangent.astype(jnp.float32) * token_weight[:, None]).astype(jnp.bfloat16)
    hidden_cols = weight_in.shape[1]
    forward_rows = jnp.dot(tokens, weight_in, preferred_element_type=jnp.float32)
    backward_rows = contract_cols(scaled, weight_out)
    summed = lax.psum_scatter(
        jnp.concatenate([forward_rows, backward_rows], axis=1).astype(jnp.bfloat16),
        "row",
        scatter_dimension=0,
        tiled=True,
    ).astype(jnp.float32)
    act_share, slope_share = gelu_parts(summed[:, :hidden_cols])
    grad_share = (summed[:, hidden_cols:] * slope_share).astype(jnp.bfloat16)
    activation, hidden_grad = (
        lax.all_gather(act_share.astype(jnp.bfloat16), "row", axis=0, tiled=True),
        lax.all_gather(grad_share, "row", axis=0, tiled=True),
    )
    input_part = contract_cols(hidden_grad, weight_in)
    grad_tokens = lax.psum(input_part.astype(jnp.bfloat16), "col")
    first_grad = contract_rows(tokens, hidden_grad)
    second_grad = contract_rows(scaled, activation)
    summed_grads = lax.psum_scatter(
        jnp.concatenate([first_grad, second_grad], axis=1).astype(jnp.bfloat16),
        "batch",
        scatter_dimension=0,
        tiled=True,
    ).astype(jnp.float32)
    grad_in = summed_grads[:, :hidden_cols].astype(jnp.bfloat16)
    grad_out = summed_grads[:, hidden_cols:].T.astype(jnp.bfloat16)
    return (grad_tokens, grad_in, grad_out)


def low(x):
    return x.astype(jnp.bfloat16)


def wide(x):
    return x.astype(jnp.float32)


def swap(x, axis, mask):
    size = lax.axis_size(axis)
    return lax.ppermute(x, axis, [(i, i ^ mask) for i in range(size)])


def call(kernel, outs, grid, in_specs, out_specs, scratch=(), scalars=1, aliases=None):
    def run(args, after):
        first, waits, results = len(in_specs) + scalars, len(after), len(outs)

        def body(*refs):
            refs = refs[:first] + refs[first + waits :]
            kernel(*refs[: first + results], *refs[first + results + 1 :])

        anywhere = pl.BlockSpec(memory_space=pl.ANY)
        return pl.pallas_call(
            body,
            out_shape=[jax.ShapeDtypeStruct(x, jnp.bfloat16) if isinstance(x, tuple) else x for x in [*outs, (16, 128)]],
            grid_spec=pltpu.PrefetchScalarGridSpec(
                num_scalar_prefetch=scalars,
                grid=grid,
                in_specs=[*in_specs] + [anywhere] * waits,
                out_specs=[*out_specs, anywhere],
                scratch_shapes=list(scratch),
            ),
            input_output_aliases=aliases or {},
            compiler_params=pltpu.CompilerParams(vmem_limit_bytes=VMEM_BYTES, has_side_effects=True),
            cost_estimate=pl.CostEstimate(flops=KERNEL_FLOPS, bytes_accessed=0, transcendentals=0),
        )(*args, *after)

    return run


def start_all(copies):
    for copy in copies:
        copy.start()
    for copy in copies:
        copy.wait()


def release_kernel(*refs):
    pass


def release(after, *arrays):
    anywhere = pl.BlockSpec(memory_space=pl.ANY)
    count = len(arrays)
    return call(
        release_kernel,
        [jax.ShapeDtypeStruct(x.shape, x.dtype) for x in arrays],
        (1,),
        [anywhere] * count,
        [anywhere] * count,
        scalars=0,
        aliases={i: i for i in range(count)},
    )(arrays, after)


def picked_copies(place, held, pieces, offsets, sems):
    block = held.shape[1] // 4
    copies, start, column = [], 0, 0
    for piece in pieces:
        filled = 0
        while filled < piece.shape[1]:
            count = min(piece.shape[1] - filled, block - column % block)
            source = (place[1] ^ offsets[column // block]) * block + column % block
            copies.append(
                pltpu.make_async_copy(
                    held.at[:, pl.ds(pl.multiple_of(source, 128), count)],
                    piece.at[:, pl.ds(filled, count)],
                    sems.at[len(copies)],
                )
            )
            filled, column = filled + count, column + count
    return copies


def partial_kernel(steps, offsets, place, left, right, weight_in, weight_out, own_pre, own_back, sent_pre, *refs):
    sent_back, picked, (held_left, held_right, sems, pick_sems) = refs[0], refs[1:-4], refs[-4:]
    step = pl.program_id(0)
    share = own_pre.shape[0]
    copies = [
        pltpu.make_async_copy(left, held_left, sems.at[0]),
        pltpu.make_async_copy(right, held_right, sems.at[1]),
    ]
    pieces = len(picked) // 2
    picks = [
        picked_copies(place, held_left, picked[:pieces], offsets[0], pick_sems.at[0]),
        picked_copies(place, held_right, picked[pieces:], offsets[1], pick_sems.at[1]),
    ]

    def store(product, own, sent):
        mine = place[0] == 0
        own[...] = low(jnp.where(mine, product[:share], product[share:]))
        sent[...] = low(jnp.where(mine, product[share:], product[:share]))

    @pl.when(step == 0)
    def _():
        copies[0].start()
        copies[1].start()
        copies[0].wait()
        for copy in picks[0]:
            copy.start()

    @pl.when(step == steps)
    def _():
        copies[1].wait()
        for copy in picks[1]:
            copy.start()

    @pl.when(step < steps)
    def _():
        store(jnp.dot(held_left[...], weight_in[...], preferred_element_type=jnp.float32), own_pre, sent_pre)

    @pl.when(step >= steps)
    def _():
        store(contract_cols(held_right[...], weight_out[...]), own_back, sent_back)

    @pl.when(step == 2 * steps - 1)
    def _():
        for copy in picks[0] + picks[1]:
            copy.wait()


def partial_products(after, place, left, right, weight_in, weight_out, first, chunk, tile, offsets, widths):
    rows, width = left.shape
    steps, base = chunk // tile, first // tile
    early = pl.BlockSpec((rows // 2, tile), lambda j, c: (0, jnp.minimum(j, steps - 1)))
    late = pl.BlockSpec((rows // 2, tile), lambda j, c: (0, jnp.maximum(j - steps, 0)))
    anywhere = pl.BlockSpec(memory_space=pl.ANY)
    return call(
        functools.partial(partial_kernel, steps, offsets),
        [(rows // 2, chunk)] * 4 + [(rows, count) for count in widths] * 2,
        (2 * steps,),
        [
            anywhere,
            anywhere,
            pl.BlockSpec((width, tile), lambda j, c: (0, base + jnp.minimum(j, steps - 1))),
            pl.BlockSpec((tile, width), lambda j, c: (base + jnp.maximum(j - steps, 0), 0)),
        ],
        [early, late, early, late] + [anywhere] * (2 * len(widths)),
        [
            pltpu.VMEM((rows, width), jnp.bfloat16),
            pltpu.VMEM((rows, width), jnp.bfloat16),
            pltpu.SemaphoreType.DMA((2,)),
            pltpu.SemaphoreType.DMA((2, 8)),
        ],
    )((place, left, right, weight_in, weight_out), after)


def hidden_kernel(pre_near, back_near, pre_sent, back_sent, act, grad):
    pre_act = wide(pre_near[...]) + wide(pre_sent[...])
    back_grad = wide(back_near[...]) + wide(back_sent[...])
    activation, slopes = gelu_parts(pre_act)
    act[...] = low(activation)
    grad[...] = low(back_grad * slopes)


def hidden(after, pre_near, back_near, pre_sent, back_sent):
    rows, cols = pre_near.shape
    step = rows // 4
    spec = pl.BlockSpec((step, cols), lambda j: (j, 0))
    return call(
        hidden_kernel,
        [(rows, cols)] * 2,
        (rows // step,),
        [spec] * 4,
        [spec] * 2,
        scalars=0,
    )((pre_near, back_near, pre_sent, back_sent), after)


def input_kernel(n_chunks, steps, place, *refs):
    shares, weight, refs = refs[: 2 * n_chunks], refs[2 * n_chunks], refs[2 * n_chunks + 1 :]
    outs, (held, sems) = refs[:-2], refs[-2:]
    share = shares[0].shape[0]
    firsts = [sum(ref.shape[1] for ref in shares[:i]) for i in range(n_chunks)]
    step, each = pl.program_id(0), len(outs) // steps

    @pl.when(step == 0)
    def _():
        copies = []
        for i, ref in enumerate(shares):
            row = place[0] if i < n_chunks else 1 - place[0]
            rows = pl.ds(pl.multiple_of(row * share, share), share)
            cols = pl.ds(firsts[i % n_chunks], ref.shape[1])
            copies.append(pltpu.make_async_copy(ref, held.at[rows, cols], sems.at[i]))
        start_all(copies)

    part = low(contract_cols(held[...], weight[...]))
    if not each:
        outs[0][...] = part
        return
    cols = part.shape[1] // each
    for i in range(steps):

        @pl.when(step == i)
        def _(i=i):
            for k in range(each):
                outs[i * each + k][...] = part[:, k * cols : (k + 1) * cols]


def input_part(after, place, near, other, weight, first, pieces, each, cols):
    share = near[0].shape[0]
    n_chunks = len(near)
    rows, width = 2 * share, sum(x.shape[1] for x in near)
    steps = pieces // each
    if pieces == 1:
        tile = 512
        return call(
            functools.partial(input_kernel, n_chunks, cols // tile),
            [(rows, cols)],
            (cols // tile,),
            [pl.BlockSpec(memory_space=pl.ANY)] * (2 * n_chunks)
            + [pl.BlockSpec((tile, width), lambda j, c: (j, 0))],
            [pl.BlockSpec((rows, tile), lambda j, c: (0, j))],
            [pltpu.VMEM((rows, width), jnp.bfloat16), pltpu.SemaphoreType.DMA((2 * n_chunks,))],
        )((place, *near, *other, weight), after)
    return call(
        functools.partial(input_kernel, n_chunks, steps),
        [(rows, cols)] * pieces,
        (steps,),
        [pl.BlockSpec(memory_space=pl.ANY)] * (2 * n_chunks)
        + [pl.BlockSpec((cols * each, width), lambda j, c: (first // each + j, 0))],
        [pl.BlockSpec((rows, cols), lambda j, c: (0, 0))] * pieces,
        [pltpu.VMEM((rows, width), jnp.bfloat16), pltpu.SemaphoreType.DMA((2 * n_chunks,))],
    )((place, *near, *other, weight), after)


def gather_hidden(offsets, first, place, shares, near, far, held, sides, sems):
    share, rows = shares[0].shape[0], near.shape[0]
    block = sides.shape[1] // 2
    copies = []

    def add(source, target):
        copies.append(pltpu.make_async_copy(source, target, sems.at[len(copies)]))

    for i, ref in enumerate(shares):
        row = place[0] if i % 2 == 0 else 1 - place[0]
        row = pl.multiple_of((2 * (i // 2) + row) * share, share)
        add(ref.at[:, pl.ds(first, held.shape[1])], held.at[pl.ds(row, share)])
    if not far:
        add(near, sides)
        return copies
    for i, offset in enumerate(offsets):
        column = pl.multiple_of((place[1] ^ offset) * block, block)
        add(near.at[:, pl.ds(column, block)], sides.at[pl.ds(0, rows), pl.ds(i * block, block)])
    column = 0
    for ref in far:
        add(ref, sides.at[pl.ds(rows, rows), pl.ds(column, ref.shape[1])])
        column += ref.shape[1]
    return copies


def weigh(sides, weight):
    step = 256

    def body(i, carry):
        rows = pl.ds(pl.multiple_of(i * step, step), step)
        sides[rows, :] = low(wide(sides[rows, :]) * weight[rows, :])
        return carry

    lax.fori_loop(0, sides.shape[0] // step, body, 0)


def weight_kernel(offsets, first, count, by_rows, place, a, b, c, d, near, *refs):
    far, weight = refs[: max(count - 1, 0)], refs[count - 1] if count else None
    sent, own, *kept = refs[count:-4] if count else refs[:-4]
    held, sides, sems, kept_sem = refs[-4:]
    step, last_step = pl.program_id(0), pl.num_programs(0) - 1
    keep = pltpu.make_async_copy(sides, kept[0], kept_sem) if kept else None

    @pl.when(step == 0)
    def _():
        start_all(gather_hidden(offsets, first, place, (a, b, c, d), near, far, held, sides, sems))
        if count:
            weigh(sides, weight)
            keep.start()

    if by_rows:
        block = sent.shape[1]

        @pl.when(step == 0)
        def _():
            sent[...] = low(contract_rows(held[...], sides[:, :block]))

        @pl.when(step == 1)
        def _():
            own[...] = low(contract_rows(held[...], sides[:, block:]))

    else:
        block, tile = sent.shape
        cols = pl.ds(pl.multiple_of(step * tile, tile), tile)
        product = contract_rows(sides[...], held[:, cols])
        sent[...] = low(product[:block])
        own[...] = low(product[block:])

    if count:

        @pl.when(step == last_step)
        def _():
            keep.wait()


def weight_part(after, place, shares, near, far, weight, offsets, first, chunk, block, tile):
    share = shares[0].shape[0]
    anywhere = pl.BlockSpec(memory_space=pl.ANY)
    if tile:
        outs, grid = [(block, chunk)] * 2, (chunk // tile,)
        out_specs = [pl.BlockSpec((block, tile), lambda j, c: (0, j))] * 2
    else:
        outs, grid = [(chunk, block)] * 2, (2,)
        out_specs = [pl.BlockSpec((chunk, block), lambda j, c: (0, 0))] * 2
    args, in_specs = [place, *shares, near], [anywhere] * 5
    both = (4 * share, 2 * block)
    count = len(far) + 1 if far else 0
    if far:
        args += [*far, weight]
        in_specs += [anywhere] * len(far) + [pl.BlockSpec(weight.shape, lambda j, c: (0, 0))]
        outs, out_specs = [*outs, both], [*out_specs, anywhere]
    return call(
        functools.partial(weight_kernel, offsets, first, count, not tile),
        outs,
        grid,
        in_specs,
        out_specs,
        [
            pltpu.VMEM((4 * share, chunk), jnp.bfloat16),
            pltpu.VMEM(both, jnp.bfloat16),
            pltpu.SemaphoreType.DMA((6 + len(far),)),
            pltpu.SemaphoreType.DMA,
        ],
    )(args, after)


def line_kernel(jobs, *refs):
    at_end, refs = refs[0], list(refs[1:])
    ins = [refs.pop(0) for _ in range(2 * len(jobs))]
    if len(refs) > len(jobs):
        refs.pop(0)
    for i, job in enumerate(jobs):
        left, right = ins[2 * i][...], ins[2 * i + 1][...]
        if job == "last":
            refs[i][...] = jnp.where(at_end[0] == 1, right, left)
        else:
            refs[i][...] = low(wide(left) + wide(right))


def line_step(after, at_end, jobs, index, buffer, width):
    names = sorted(jobs)
    rows, cols = next(iter(jobs.values()))[0].shape
    step = rows // LINE_STEPS
    spec = pl.BlockSpec((step, cols), lambda j, c: (j, 0))
    outs, out_specs, args, aliases, in_specs = [], [], [at_end], {}, []
    for i, name in enumerate(names):
        args += jobs[name]
        in_specs += [spec, spec]
        if name == "last":
            outs.append((rows, width))
            out_specs.append(pl.BlockSpec((step, cols), lambda j, c: (j, index)))
        else:
            outs.append((rows, cols))
            out_specs.append(spec)
    if "last" in jobs and buffer is not None:
        aliases = {len(args): names.index("last")}
        args.append(buffer)
        in_specs.append(pl.BlockSpec(memory_space=pl.ANY))
    *results, mark = call(
        functools.partial(line_kernel, names), outs, (LINE_STEPS,), in_specs, out_specs, aliases=aliases
    )(args, after)
    return dict(zip(names, results)), mark


def sum_kernel(left, right, *refs):
    refs[-1][...] = low(wide(left[...]) + wide(right[...]))


def sum_into(after, left, right, buffer, shape, index, by_rows):
    rows, cols = left.shape
    steps = 4
    step = rows // steps
    spec = pl.BlockSpec((step, cols), lambda j: (j, 0))
    if by_rows:
        out = pl.BlockSpec((step, cols), lambda j: (index * steps + j, 0))
    else:
        out = pl.BlockSpec((step, cols), lambda j: (j, index))
    args, in_specs, aliases = [left, right], [spec, spec], {}
    if buffer is not None:
        args.append(buffer)
        in_specs.append(pl.BlockSpec(memory_space=pl.ANY))
        aliases = {2: 0}
    return call(sum_kernel, [shape], (steps,), in_specs, [out], scalars=0, aliases=aliases)(args, after)


def per_device(tokens, cotangent, weight_in, weight_out, segment_ids, keep_mask):
    sizes = tuple(lax.axis_size(axis) for axis in ("batch", "row", "col"))
    if sizes != (4, 2, 4) or weight_in.shape[1] % 1536 or tokens.shape[1] % (256 * PIECES // 2):
        return per_device_any(tokens, cotangent, weight_in, weight_out, segment_ids, keep_mask)
    here, row, col = (lax.axis_index(axis) for axis in ("batch", "row", "col"))
    rows, width = tokens.shape
    hidden_cols = weight_in.shape[1]
    block, share = width // 4, rows // 2
    chunks = (hidden_cols // 3 * 2, hidden_cols // 3)
    firsts = (0, chunks[0])
    place = jnp.stack([row, here]).astype(jnp.int32)
    at_end = ((col == 0) | (col == 3)).astype(jnp.int32).reshape(1)

    last = []

    def chain(run, *args, needs=()):
        *results, mark = run([*last, *needs], *args)
        last[:] = [mark]
        return results

    count = len(chunks)
    partial, act_own, grad_own, act_other, grad_other = ([None] * count for _ in range(5))
    act_far, grad_far, act_swap, grad_swap = ([None] * count for _ in range(4))

    tokens_far, cot_far = [], []

    def forward(i, widths=(), needs=()):
        own_pre, own_back, sent_pre, sent_back, *picked = chain(
            partial_products,
            place,
            tokens,
            cotangent,
            weight_in,
            weight_out,
            firsts[i],
            chunks[i],
            512,
            ((3, 1), (3, 2)),
            widths,
            needs=needs,
        )
        partial[i] = (own_pre, own_back, swap(sent_pre, "row", 1), swap(sent_back, "row", 1))
        if picked:
            tokens_far.extend(swap(x, "batch", 1) for x in picked[: len(widths)])
            cot_far.extend(swap(x, "batch", 2) for x in picked[len(widths) :])

    def activate(i, needs=()):
        act, grad = chain(hidden, *partial[i], needs=needs)
        act_own[i], grad_own[i] = act, grad
        grad_other[i], act_other[i] = swap(grad, "row", 1), swap(act, "row", 1)

    def send(i, needs=()):
        if needs:
            grad_own[i], act_own[i] = chain(release, grad_own[i], act_own[i], needs=needs)
        grad_far[i], act_far[i] = swap(grad_own[i], "batch", 1), swap(act_own[i], "batch", 2)

    def exchange(i, needs=()):
        grad_far[i], act_far[i] = chain(release, grad_far[i], act_far[i], needs=needs)
        grad_swap[i], act_swap[i] = swap(grad_far[i], "row", 1), swap(act_far[i], "row", 1)

    cols = width // PIECES
    parts, inward = [], []
    half, across, total, outward = ([None] * PIECES for _ in range(4))
    grad_tokens = None

    def inputs(pieces, needs=()):
        made = chain(
            input_part, place, grad_own, grad_other, weight_in, len(parts), pieces, 2, cols, needs=needs
        )
        parts.extend(made)
        inward.extend(lax.ppermute(x, "col", [(0, 1), (3, 2)]) for x in made)

    def line(first=None, second=None, third=None, needs=()):
        nonlocal grad_tokens
        jobs = {}
        if first is not None:
            jobs["half"] = (parts[first], inward[first])
        if second is not None:
            jobs["total"] = (half[second], across[second])
        if third is not None:
            jobs["last"] = (total[third], outward[third])
        made, mark = line_step([*last, *needs], at_end, jobs, third, grad_tokens, width)
        last[:] = [mark]
        if first is not None:
            half[first] = made["half"]
            across[first] = lax.ppermute(half[first], "col", [(1, 2), (2, 1)])
        if second is not None:
            total[second] = made["total"]
            outward[second] = lax.ppermute(total[second], "col", [(1, 0), (2, 3)])
        grad_tokens = made.get("last", grad_tokens)

    part = chunks[-1]
    places = [(i, k) for i in range(count) for k in range(chunks[i] // part)]
    in_own, out_own, in_sent, out_sent = ([None] * len(places) for _ in range(4))

    sides = {}

    def weights(name, n, shares, near, far, weight, offsets, tile, mask):
        near, far = (sides[name], ()) if name in sides else (near, far)
        first = places[n][1] * part
        sent, own, *kept = chain(weight_part, place, shares, near, far, weight, offsets, first, part, block, tile)
        if kept:
            (sides[name],) = kept
        return own, swap(sent, "batch", mask)

    def weights_in(n):
        i = places[n][0]
        shares = (grad_own[i], grad_other[i], grad_far[i], grad_swap[i])
        in_own[n], in_sent[n] = weights("in", n, shares, tokens, tokens_far, weight_in_pair, (2, 0), 512, 2)

    def weights_out(n):
        i = places[n][0]
        shares = (act_own[i], act_other[i], act_far[i], act_swap[i])
        out_own[n], out_sent[n] = weights("out", n, shares, cotangent, cot_far, weight_out_pair, (1, 0), 0, 1)

    grad_in = grad_out = None

    def finish(i):
        nonlocal grad_in, grad_out
        (grad_in,) = chain(sum_into, in_own[i], in_sent[i], grad_in, (block, hidden_cols), i, False)
        (grad_out,) = chain(sum_into, out_own[i], out_sent[i], grad_out, (hidden_cols, block), i, True)

    early = (2 * block * 5 // 12) // 128 * 128
    forward(0, (early, 2 * block - early))
    forward(1)
    activate(0)
    activate(1, needs=[tokens_far[0], cot_far[0]])
    send(0)
    (summand,) = chain(input_part, place, grad_own, grad_other, weight_in, 0, 1, 1, width)
    total = lax.psum(summand, "col")
    exchange(0, needs=[tokens_far[1], cot_far[1]])

    (marks,) = chain(release, jnp.stack([segment_ids, keep_mask]))
    marks = lax.all_gather(marks, "batch")
    image_sizes = sum(image_counts(*marks[i]) for i in range(4))
    token_weight, weight_x, weight_y = (
        image_weights(*lax.dynamic_index_in_dim(marks, here ^ k, keepdims=False), image_sizes)[:, None]
        for k in range(3)
    )
    weight_in_pair = jnp.concatenate([token_weight, weight_x], axis=0)
    weight_out_pair = jnp.concatenate([token_weight, weight_y], axis=0)
    grad_tokens = low(wide(total) * token_weight)
    send(1, needs=[weight_in_pair, weight_out_pair])
    weights_out(0)
    weights_in(0)
    weights_out(1)
    exchange(1)
    weights_in(1)
    weights_out(2)
    finish(0)
    weights_in(2)
    finish(1)
    finish(2)
    return (grad_tokens, grad_in, grad_out)


def solution(mesh):
    return jax.shard_map(
        per_device,
        mesh=mesh,
        in_specs=(
            P("batch", "row"),
            P("batch", "row"),
            P("row", "col"),
            P("col", "row"),
            P("batch"),
            P("batch"),
        ),
        out_specs=(P("batch", "row"), P(("row", "batch"), "col"), P("col", ("row", "batch"))),
        check_vma=False,
    )
```
